128 devices in a mesh: row: 8 (over x, core), col: 16 (over y, z).
Axes of the slice: x: 4, y: 4, z: 4, core: 2. Of those that a mesh axis runs over, the one named last changes fastest.
Arguments:
- object_field: float32 [2, 4096, 8192], P(None, 'row', 'col'), may hold values from -5 to 5
- probe: float32 [2, 2, 256, 256], replicated, may hold values from -5 to 5
- amplitudes: float32 [1024, 256, 256], P(('row', 'col')), may hold values from 0 to 2.5
- positions: int32 [1024, 2], P(('row', 'col')), may hold values from 0 to 7936, as said below
- counts: int32 [128], P(('row', 'col')), may hold values from 1 to 8, as said below
Outputs:
- new_object: float32 [2, 4096, 8192], P(None, 'row', 'col')
- new_probe: float32 [2, 2, 256, 256], replicated
The draws below stay inside these ranges and needn't reach their ends.
Inputs may be any that keep to these rules, and one draw needn't show every extreme that they name: `positions`: each slot's patch lies inside the object, and its top-left pixel lies in the tile of the device that holds the slot. `counts`: one device holds exactly 8 live slots in every draw; the others fewer.
All inputs are finite; a program needn't handle non-finite values.
Results may differ from the reference program's by a relative error of at most 0.0003.
Values sent between devices are 32-bit elements; how exact they have to be, the bound alone decides.
A program may use at most 256 MiB of HBM per device.

```python
import jax
import jax.numpy as jnp
from jax import lax

P_SIZE = 256
M = 2
TH = 512
TW = 512
CAP = 8
NY = 4096
NX = 8192
SLOTS = 1024
N_ROW = 8
N_COL = 16


def draw_counts(key, part):
    key = jax.random.fold_in(key, 11)
    first, second = jax.random.split(key)
    devices_all = N_ROW * N_COL
    base = jax.random.randint(first, (devices_all,), max(1, CAP // 4), CAP // 2 + 1, dtype=jnp.int32)
    busiest = jax.random.randint(second, (), 0, devices_all, dtype=jnp.int32)
    return jnp.where(jnp.arange(devices_all, dtype=jnp.int32) == busiest, CAP, base).astype(jnp.int32)


def draw_positions(key, part):
    key = jax.random.fold_in(key, 23)
    first, second = jax.random.split(key)
    slot_ids = jnp.arange(SLOTS, dtype=jnp.int32)
    device = slot_ids // CAP
    tile_row = device // N_COL
    tile_col = device % N_COL
    rows = tile_row * TH + jax.random.randint(first, (SLOTS,), 0, TH, dtype=jnp.int32)
    cols = tile_col * TW + jax.random.randint(second, (SLOTS,), 0, TW, dtype=jnp.int32)
    rows = jnp.minimum(rows, NY - P_SIZE)
    cols = jnp.minimum(cols, NX - P_SIZE)
    return jnp.stack([rows, cols], axis=1).astype(jnp.int32)


def block_levels(stream_key, dims, cuts, least, largest):
    def one(dim, parts):
        steps = jax.random.uniform(jax.random.fold_in(jax.random.fold_in(stream_key, 6), dim), (parts,), jnp.float32, least / len(cuts), largest / len(cuts))
        return jnp.repeat(jnp.exp(steps), dims[dim] // parts).reshape((-1,) + (1,) * (len(dims) - dim - 1))

    level = one(*cuts[0])
    for cut in cuts[1:]:
        level = level * one(*cut)
    return level


def gaussian(rng, dims, scale, limit, pieces=(), kind=jnp.bfloat16):
    array = scale * jax.random.normal(rng, dims, jnp.float32)
    if pieces:
        array = array * block_levels(rng, dims, pieces, -0.22, 0.18)
    return jnp.clip(array, -limit, limit).astype(kind)


def setup_inputs(seed: int = 0) -> dict:
    seeds = jax.random.split(jax.random.key(seed), 6)
    object_field = gaussian(seeds[0], (2, NY, NX), 0.7, 5.0, ((1, 8), (2, 16)), jnp.float32)
    probe = gaussian(seeds[1], (M, 2, P_SIZE, P_SIZE), 0.7, 5.0, (), jnp.float32)
    amplitudes = jnp.clip(2.5 * jax.random.uniform(seeds[2], (SLOTS, P_SIZE, P_SIZE), jnp.float32) ** block_levels(seeds[2], (SLOTS, P_SIZE, P_SIZE), ((0, 128),), -0.2, 0.2), 0.0, 2.5)
    positions = draw_positions(jax.random.fold_in(seeds[5], 71), 0)
    counts = draw_counts(jax.random.fold_in(seeds[5], 71), 0)
    return {"object_field": object_field, "probe": probe, "amplitudes": amplitudes, "positions": positions, "counts": counts}


def pattern_terms(patch, probe, amplitude):
    patch_c = patch[0] + 1j * patch[1]
    probe_c = probe[:, 0] + 1j * probe[:, 1]
    exit_wave = probe_c * patch_c[None]
    far_field = jnp.fft.fft2(exit_wave, norm='ortho')
    intensity = lax.optimization_barrier(jnp.sum(jnp.real(far_field) ** 2 + jnp.imag(far_field) ** 2, axis=0))
    factor = amplitude / jnp.maximum(jnp.sqrt(intensity), 0.3) - 1.0
    back_wave = jnp.fft.ifft2(far_field * factor[None], norm='ortho')
    object_grad = lax.optimization_barrier(jnp.sum(jnp.conj(probe_c) * back_wave, axis=0))
    object_light = lax.optimization_barrier(jnp.sum(probe[:, 0] ** 2 + probe[:, 1] ** 2, axis=0))
    object_terms = jnp.stack([jnp.real(object_grad), jnp.imag(object_grad), object_light])
    probe_grad = jnp.conj(patch_c)[None] * back_wave
    probe_terms = jnp.stack([jnp.real(probe_grad), jnp.imag(probe_grad)], axis=1)
    probe_light = patch[0] ** 2 + patch[1] ** 2
    return (object_terms, probe_terms, probe_light)

def reference(object_field, probe, amplitudes, positions, counts):
    slot_ids = jnp.arange(SLOTS, dtype=jnp.int32)
    live = (slot_ids % CAP < counts[slot_ids // CAP]).astype(jnp.float32)
    zero_index = jnp.zeros((), jnp.int32)

    def visit(carry, inputs):
        grid, probe_sum, light_sum = carry
        amplitude, position, weight = inputs
        top = position[0].astype(jnp.int32)
        left = position[1].astype(jnp.int32)
        patch = lax.dynamic_slice(object_field, (zero_index, top, left), (2, P_SIZE, P_SIZE))
        object_terms, probe_terms, probe_light = pattern_terms(patch, probe, amplitude)
        current = lax.dynamic_slice(grid, (zero_index, top, left), (3, P_SIZE, P_SIZE))
        grid = lax.dynamic_update_slice(grid, current + weight * object_terms, (zero_index, top, left))
        return ((grid, probe_sum + weight * probe_terms, light_sum + weight * probe_light), None)
    start = (jnp.zeros((3, NY, NX), jnp.float32), jnp.zeros((M, 2, P_SIZE, P_SIZE), jnp.float32), jnp.zeros((P_SIZE, P_SIZE), jnp.float32))
    (grid, probe_sum, light_sum), _ = lax.scan(visit, start, (amplitudes, positions, live))
    new_object = object_field + grid[:2] / (grid[2] + 1.0)
    new_probe = probe + probe_sum / (light_sum + 1.0)
    return (new_object, new_probe)
```

```python
import functools

import jax
import jax.numpy as jnp
import ml_dtypes
import numpy as np
from jax import lax
from jax.experimental import pallas as pl
from jax.experimental.pallas import tpu as pltpu
from jax.sharding import PartitionSpec as P

SIDE = 256
HALF = 128
MODES = 2
CHUNK = 32
VMEM_LIMIT = 56 * 1024 * 1024


def dft_tables():
    point = np.arange(HALF)[:, None]
    right, left = [], []
    for odd in (0, 1):
        angle = 2.0 * np.pi * ((point * (2 * np.arange(HALF)[None, :] + odd)) % SIDE) / SIDE
        cosine, sine = np.cos(angle) / 16.0, np.sin(angle) / 16.0
        table = np.block([[cosine, -sine], [sine, cosine]]).astype(np.float32)
        high = table.astype(ml_dtypes.bfloat16)
        low = (table - high.astype(np.float32)).astype(ml_dtypes.bfloat16)
        right += [np.concatenate([high, high, low], 0), np.concatenate([high.T, high.T, low.T], 0)]
        left += [np.concatenate([high.T, low.T, high.T], 1), np.concatenate([high, low, high], 1)]
    return np.stack(right), np.stack(left)


def split(value):
    high = value.astype(jnp.bfloat16)
    return high, (value - high.astype(jnp.float32)).astype(jnp.bfloat16)


def dot(left, right):
    return jnp.dot(left, right, preferred_element_type=jnp.float32)


def part(index):
    return pl.ds(index * HALF, HALF)


def pattern_kernel(
    span, order, corners, tile, right_upper, right_lower, lower_rim, corner_rim, probe, amplitude,
    right_table, left_table, grid, probe_sum,
    extended, sems, patch, rows_in, rows_out, columns_in, columns_out,
):
    copies = []
    for c in range(2):
        for j in range(6):
            if j < 4:
                pieces = ((tile, 0, 512), (lower_rim, 512, 256))
            else:
                pieces = ((right_upper, 0, 256), (right_lower, 256, 256), (corner_rim, 512, 256))
            for source, row, rows in pieces:
                copies.append((source.at[c, :, part(j % 4)], extended.at[c, j, pl.ds(row, rows)]))
    copies = [pltpu.make_async_copy(a, b, sems.at[k]) for k, (a, b) in enumerate(copies)]
    for copy in copies:
        copy.start()
    grid[...] = jnp.zeros_like(grid)
    probe_sum[...] = jnp.zeros_like(probe_sum)
    for copy in copies:
        copy.wait()

    lane = lax.broadcasted_iota(jnp.int32, (CHUNK, HALF), 1)

    def visit(step, carry):
        slot = order[step]
        top = corners[slot, 0]
        left = corners[slot, 1]
        first = left // HALF
        shift = lax.rem(left, HALF)
        back_shift = lax.rem(HALF - shift, HALF)

        def load(step, carry):
            r = pl.multiple_of(step * CHUNK, CHUNK)
            rows = pl.ds(r, CHUNK)
            pixels = []
            for c in range(2):
                tiles = [
                    pltpu.roll(extended[c, first + j, pl.ds(top + r, CHUNK), :], back_shift, 1) for j in range(3)
                ]
                pair = [jnp.where(lane < HALF - shift, tiles[j], tiles[j + 1]) for j in range(2)]
                for j in range(2):
                    patch[c, rows, part(j)] = pair[j]
                pixels.append(pair)
            for j in range(2):
                probe_sum[4, pl.ds(j * SIDE + r, CHUNK), :] += pixels[0][j] * pixels[0][j] + pixels[1][j] * pixels[1][j]
            for m in range(MODES):
                real, imag = [], []
                for j in range(2):
                    probe_real, probe_imag = probe[m, 0, rows, part(j)], probe[m, 1, rows, part(j)]
                    real.append(probe_real * pixels[0][j] - probe_imag * pixels[1][j])
                    imag.append(probe_real * pixels[1][j] + probe_imag * pixels[0][j])
                at = pl.ds(pl.multiple_of(m * SIDE + r, CHUNK), CHUNK)
                for k, (first_half, second_half) in enumerate((real, imag)):
                    for odd, value in enumerate((first_half + second_half, first_half - second_half)):
                        high, low = split(value)
                        rows_in[odd, at, part(k)] = high
                        rows_in[odd, at, part(2 + k)] = low
            return carry

        lax.fori_loop(0, SIDE // CHUNK, load, 0, unroll=True)

        def along_rows(inverse):
            for odd in range(2):
                cut = rows_in[odd]
                cut = jnp.concatenate([cut, cut[:, :SIDE]], axis=1)
                rows_out[odd] = dot(cut, right_table[2 * odd + inverse])

        def along_columns(inverse):
            for odd in range(2):
                high, low = columns_in[odd, 0], columns_in[odd, 1]
                cut = jnp.concatenate([high, high, low], axis=0)
                columns_out[odd] = dot(left_table[2 * odd + inverse], cut)

        along_rows(0)

        def turn(step, carry):
            r = pl.multiple_of(step * CHUNK, CHUNK)
            for m in range(MODES):
                for odd in range(2):
                    for k in range(2):
                        upper = rows_out[odd, pl.ds(m * SIDE + r, CHUNK), part(k)]
                        lower = rows_out[odd, pl.ds(m * SIDE + HALF + r, CHUNK), part(k)]
                        for q, value in enumerate((upper + lower, upper - lower)):
                            high, low = split(value)
                            columns_in[q, 0, pl.ds(k * HALF + r, CHUNK), part(2 * m + odd)] = high
                            columns_in[q, 1, pl.ds(k * HALF + r, CHUNK), part(2 * m + odd)] = low
            return carry

        lax.fori_loop(0, HALF // CHUNK, turn, 0, unroll=True)
        along_columns(0)

        def scale(step, carry):
            r = pl.multiple_of(step * CHUNK, CHUNK)
            for q in range(2):
                for odd in range(2):
                    values = [
                        [columns_out[q, pl.ds(k * HALF + r, CHUNK), part(2 * m + odd)] for k in range(2)]
                        for m in range(MODES)
                    ]
                    intensity = sum(v * v for pair in values for v in pair)
                    measured = amplitude[slot, pl.ds(q * HALF + r, CHUNK), part(odd)]
                    factor = measured * lax.rsqrt(jnp.maximum(intensity, 0.09)) - 1.0
                    for m in range(MODES):
                        for k in range(2):
                            high, low = split(values[m][k] * factor)
                            columns_in[q, 0, pl.ds(k * HALF + r, CHUNK), part(2 * m + odd)] = high
                            columns_in[q, 1, pl.ds(k * HALF + r, CHUNK), part(2 * m + odd)] = low
            return carry

        lax.fori_loop(0, HALF // CHUNK, scale, 0, unroll=True)
        along_columns(1)

        def turn_back(step, carry):
            r = pl.multiple_of(step * CHUNK, CHUNK)
            for m in range(MODES):
                for odd in range(2):
                    for k in range(2):
                        even_sum = columns_out[0, pl.ds(k * HALF + r, CHUNK), part(2 * m + odd)]
                        odd_sum = columns_out[1, pl.ds(k * HALF + r, CHUNK), part(2 * m + odd)]
                        for q, value in enumerate((even_sum + odd_sum, even_sum - odd_sum)):
                            high, low = split(value)
                            at = pl.ds(m * SIDE + q * HALF + r, CHUNK)
                            rows_in[odd, at, part(k)] = high
                            rows_in[odd, at, part(2 + k)] = low
            return carry

        lax.fori_loop(0, HALF // CHUNK, turn_back, 0, unroll=True)
        along_rows(1)

        def gather(step, carry):
            r = pl.multiple_of(step * CHUNK, CHUNK)
            rows = pl.ds(r, CHUNK)
            real_grad, imag_grad = [0.0, 0.0], [0.0, 0.0]
            for m in range(MODES):
                at = pl.ds(pl.multiple_of(m * SIDE + r, CHUNK), CHUNK)
                even = [rows_out[0, at, part(k)] for k in range(2)]
                odd = [rows_out[1, at, part(k)] for k in range(2)]
                for j in range(2):
                    real, imag = [e + o if j == 0 else e - o for e, o in zip(even, odd)]
                    patch_real, patch_imag = patch[0, rows, part(j)], patch[1, rows, part(j)]
                    probe_sum[2 * m, pl.ds(j * SIDE + r, CHUNK), :] += patch_real * real + patch_imag * imag
                    probe_sum[2 * m + 1, pl.ds(j * SIDE + r, CHUNK), :] += patch_real * imag - patch_imag * real
                    probe_real, probe_imag = probe[m, 0, rows, part(j)], probe[m, 1, rows, part(j)]
                    real_grad[j] += probe_real * real + probe_imag * imag
                    imag_grad[j] += probe_real * imag - probe_imag * real
            for c, pair in enumerate((real_grad, imag_grad)):
                here, there = [pltpu.roll(value, shift, 1) for value in pair]
                tiles = (
                    jnp.where(lane >= shift, here, 0.0),
                    jnp.where(lane >= shift, there, here),
                    jnp.where(lane >= shift, 0.0, there),
                )
                for j in range(3):
                    grid[c, first + j, pl.ds(top + r, CHUNK), :] += tiles[j]
            return carry

        lax.fori_loop(0, SIDE // CHUNK, gather, 0, unroll=True)
        return carry

    lax.fori_loop(span[0], span[1], visit, 0)


def patterns(span, order, corners, tile, right_upper, right_lower, lower_rim, corner_rim, probe, amplitude):
    right_table, left_table = dft_tables()
    smem, vmem, anywhere = [pl.BlockSpec(memory_space=s) for s in (pltpu.SMEM, pltpu.VMEM, pl.ANY)]
    return pl.pallas_call(
        pattern_kernel,
        out_shape=(
            jax.ShapeDtypeStruct((2, 6, 768, HALF), jnp.float32),
            jax.ShapeDtypeStruct((5, 2 * SIDE, HALF), jnp.float32),
        ),
        in_specs=[smem] * 3 + [anywhere] * 5 + [vmem] * 4,
        out_specs=(vmem, vmem),
        scratch_shapes=[
            pltpu.VMEM((2, 6, 768, HALF), jnp.float32),
            pltpu.SemaphoreType.DMA((28,)),
            pltpu.VMEM((2, SIDE, SIDE), jnp.float32),
            pltpu.VMEM((2, MODES * SIDE, 2 * SIDE), jnp.bfloat16),
            pltpu.VMEM((2, MODES * SIDE, SIDE), jnp.float32),
            pltpu.VMEM((2, 2, SIDE, MODES * SIDE), jnp.bfloat16),
            pltpu.VMEM((2, SIDE, MODES * SIDE), jnp.float32),
        ],
        compiler_params=pltpu.CompilerParams(vmem_limit_bytes=VMEM_LIMIT),
        cost_estimate=pl.CostEstimate(flops=5_000_000_000, bytes_accessed=20_000_000, transcendentals=0),
        name="patterns",
    )(span, order, corners, tile, right_upper, right_lower, lower_rim, corner_rim, probe, amplitude, right_table, left_table)


def prepare_kernel(corners, counts, probe, amplitude, parity, inverse_light, by_parity, canvas, power, columns):
    canvas[...] = jnp.zeros_like(canvas)
    power[...] = sum(probe[m, c] * probe[m, c] for m in range(MODES) for c in range(2))
    lane = lax.broadcasted_iota(jnp.int32, (CHUNK, HALF), 1)

    for source in range(4):

        def place(slot, carry):
            top = corners[source, slot, 0] + SIDE
            left = corners[source, slot, 1] + SIDE

            @pl.when((top > 0) & (left > 0))
            def _():
                first = left // HALF
                shift = lax.rem(left, HALF)
                for r in range(0, SIDE, CHUNK):
                    rows = pl.ds(r, CHUNK)
                    here, there = [pltpu.roll(power[rows, part(j)], shift, 1) for j in range(2)]
                    tiles = (
                        jnp.where(lane >= shift, here, 0.0),
                        jnp.where(lane >= shift, there, here),
                        jnp.where(lane >= shift, 0.0, there),
                    )
                    for j in range(3):
                        canvas[first + j, pl.ds(top + r, CHUNK), :] += tiles[j]

            return carry

        lax.fori_loop(0, counts[source], place, 0)

    for j in range(4):
        inverse_light[j] = 1.0 / (canvas[2 + j, pl.ds(SIDE, 512), :] + 1.0)

    def reorder(slot, carry):
        for j in range(2):
            columns[j] = amplitude[slot, :, part(j)]
        for q in range(2):
            value = jnp.concatenate([columns[j, pl.ds(q, HALF, stride=2), :] for j in range(2)], axis=1)
            pieces = []
            for _ in range(3):
                high = value.astype(jnp.bfloat16)
                pieces.append(high)
                value = value - high.astype(jnp.float32)
            by_parity[slot, part(q), :] = dot(jnp.concatenate(pieces, axis=1), parity[...])
        return carry

    lax.fori_loop(0, counts[0], reorder, 0)


def prepare(corners, counts, probe, amplitude):
    target = np.arange(SIDE)
    parity = (np.arange(SIDE)[:, None] == 2 * (target % HALF) + target // HALF).astype(ml_dtypes.bfloat16)
    smem, vmem = [pl.BlockSpec(memory_space=space) for space in (pltpu.SMEM, pltpu.VMEM)]
    return pl.pallas_call(
        prepare_kernel,
        out_shape=(
            jax.ShapeDtypeStruct((4, 512, HALF), jnp.float32),
            jax.ShapeDtypeStruct((8, SIDE, SIDE), jnp.float32),
        ),
        in_specs=[smem] * 2 + [vmem] * 3,
        out_specs=(vmem, vmem),
        scratch_shapes=[pltpu.VMEM((8, 1024, HALF), jnp.float32), pltpu.VMEM((SIDE, SIDE), jnp.float32), pltpu.VMEM((2, SIDE, HALF), jnp.float32)],
        compiler_params=pltpu.CompilerParams(vmem_limit_bytes=VMEM_LIMIT),
        cost_estimate=pl.CostEstimate(flops=2_000_000_000, bytes_accessed=8_000_000, transcendentals=0),
        name="prepare",
    )(corners, counts, probe, amplitude, np.concatenate([parity] * 3, 0))


def finish_kernel(
    grid, probe_sum, tile, inverse_light, probe, new_object, new_probe,
    own, own_half, inverse, old, corner_in, below_in, right_in, right_out, half_in, by_y, by_x, by_z, turned,
    local_sems, spill_send, spill_recv, half_send, half_recv, y_send, y_recv, x_send, x_recv, z_send, z_recv,
    x_back_send, x_back_recv, y_back_send, y_back_recv, last_send, last_recv,
):
    row, col = lax.axis_index("row"), lax.axis_index("col")
    x, core = row // 2, lax.rem(row, 2)
    y, z = col // 4, lax.rem(col, 4)
    sibling = (row + 1 - 2 * core, col)
    y_peers = {d: (row, lax.rem(y + d, 4) * 4 + z) for d in (1, 2, 3)}
    x_peers = {d: (lax.rem(x + d, 4) * 2 + core, col) for d in (1, 2, 3)}
    z_peers = {d: (row, y * 4 + lax.rem(z + d, 4)) for d in (1, 2, 3)}
    has_above, has_below = row > 0, row < 7
    has_left, has_right = col > 0, col < 15

    def remote(source, target, send, recv, device):
        return pltpu.make_async_remote_copy(
            src_ref=source, dst_ref=target, send_sem=send, recv_sem=recv, device_id=device,
            device_id_type=pl.DeviceIdType.MESH,
        )

    def signal(device):
        pl.semaphore_signal(barrier, inc=1, device_id=device, device_id_type=pl.DeviceIdType.MESH)

    half_at = core * 256
    loads = [
        pltpu.make_async_copy(probe_sum.at[:, pl.ds(pl.multiple_of(half_at, 256), 256)], own_half, local_sems.at[0]),
        pltpu.make_async_copy(grid.at[:, pl.ds(4, 2), pl.ds(0, 256)], right_out, local_sems.at[1]),
        pltpu.make_async_copy(grid.at[:, pl.ds(0, 4), pl.ds(0, 512)], own, local_sems.at[2]),
        pltpu.make_async_copy(inverse_light, inverse, local_sems.at[3]),
        pltpu.make_async_copy(tile, old, local_sems.at[4]),
    ]
    for load in loads:
        load.start()

    barrier = pltpu.get_barrier_semaphore()
    for device in [sibling, *y_peers.values(), *x_peers.values(), *z_peers.values()]:
        signal(device)
    steps = ((has_above, (row - 1, col)), (has_below, (row + 1, col)), (has_left, (row, col - 1)), (has_right, (row, col + 1)))
    for there, device in steps:
        pl.when(there)(functools.partial(signal, device))
    pl.semaphore_wait(barrier, 10 + sum(there.astype(jnp.int32) for there, _ in steps))

    below, right = (row + 1, col), (row, col + 1)
    corner = remote(
        grid.at[:, pl.ds(4, 2), pl.ds(512, 256)], corner_in, spill_send.at[0], spill_recv.at[0], below
    )
    right_lower = remote(
        grid.at[:, pl.ds(4, 2), pl.ds(256, 256)], right_in.at[:, :, pl.ds(256, 256)],
        spill_send.at[1], spill_recv.at[1], right,
    )
    lower = remote(grid.at[:, pl.ds(0, 4), pl.ds(512, 256)], below_in, spill_send.at[2], spill_recv.at[2], below)
    right_upper = remote(
        right_out, right_in.at[:, :, pl.ds(0, 256)], spill_send.at[3], spill_recv.at[3], right
    )

    def y_rows(d):
        return pl.ds(pl.multiple_of(lax.rem(y + d, 4) * 64, 64), 64)

    halves = {
        d: remote(
            probe_sum.at[:, pl.ds(pl.multiple_of((1 - core) * 256 + lax.rem(y + d, 4) * 64, 64), 64)],
            half_in.at[:, y_rows(d)], half_send.at[d], half_recv.at[d], sibling,
        )
        for d in range(4)
    }
    pl.when(has_below)(corner.start)
    for d in (2, 1, 3, 0):
        halves[d].start()
    pl.when(has_right)(right_lower.start)
    pl.when(has_below)(lower.start)

    loads[0].wait()
    outward = {
        d: remote(own_half.at[:, y_rows(d)], by_y.at[3 - d], y_send.at[d - 1], y_recv.at[3 - d], y_peers[d])
        for d in (1, 2, 3)
    }
    for d in (2, 1, 3, 0):
        halves[d].wait_recv()
        own_half[:, y_rows(d)] = own_half[:, y_rows(d)] + half_in[:, y_rows(d)]
        if d:
            outward[d].start()

    loads[1].wait()

    @pl.when(has_above)
    def _():
        corner.wait_recv()
        right_out[...] = right_out[...] + corner_in[...]

    pl.when(has_right)(right_upper.start)

    for d in (1, 2, 3):
        outward[d].wait_recv()
    mine = y_rows(0)
    own_half[:, mine] = own_half[:, mine] + (by_y[0] + by_y[1] + by_y[2])

    def x_rows(d, base):
        return pl.ds(pl.multiple_of(base + lax.rem(x + d, 4) * 16, 16), 16)

    crossing = {
        d: remote(own_half.at[:, x_rows(d, y * 64)], by_x.at[3 - d], x_send.at[d - 1], x_recv.at[3 - d], x_peers[d])
        for d in (1, 2, 3)
    }
    for d in (1, 2, 3):
        crossing[d].start()

    for load in loads[2:]:
        load.wait()

    def update(step, carry):
        rows = pl.ds(pl.multiple_of(step * CHUNK, CHUNK), CHUNK)
        for c in range(2):
            for j in range(4):
                new_object[c, rows, part(j)] = old[c, rows, part(j)] + own[c, j, rows] * inverse[j, rows]
        return carry

    lax.fori_loop(0, 512 // CHUNK, update, 0)

    for d in (1, 2, 3):
        crossing[d].wait_recv()
    by_z[z] = own_half[:, x_rows(0, y * 64)] + (by_x[0] + by_x[1] + by_x[2])
    along = {
        d: remote(by_z.at[z], by_z.at[z], z_send.at[d - 1], z_recv.at[3 - d], z_peers[d]) for d in (1, 2, 3)
    }
    for d in (1, 2, 3):
        along[d].start()
    for d in (1, 2, 3):
        along[d].wait_recv()
    total = (by_z[0] + by_z[1]) + (by_z[2] + by_z[3])
    light = total[4] + 1.0
    pixels = pl.ds(pl.multiple_of(y * 64 + x * 16, 16), 16)
    lanes = pl.ds(pl.multiple_of(core * HALF, HALF), HALF)
    home = x_rows(0, half_at + y * 64)
    for m in range(MODES):
        for c in range(2):
            turned[2 * m + c, home] = probe[m, c, pixels, lanes] + total[2 * m + c] / light

    back_x = {
        d: remote(turned.at[:, home], turned.at[:, home], x_back_send.at[d - 1], x_back_recv.at[3 - d], x_peers[d])
        for d in (1, 2, 3)
    }
    for d in (1, 2, 3):
        back_x[d].start()
    for d in (1, 2, 3):
        back_x[d].wait_recv()

    def quarter(d):
        return pl.ds(pl.multiple_of(half_at + lax.rem(y + d, 4) * 64, 64), 64)

    back_y = {
        d: remote(
            turned.at[:, quarter(0)], turned.at[:, quarter(0)], y_back_send.at[d - 1], y_back_recv.at[3 - d], y_peers[d]
        )
        for d in (1, 2, 3)
    }
    last = {
        d: remote(turned.at[:, quarter(d)], turned.at[:, quarter(d)], last_send.at[d], last_recv.at[d], sibling)
        for d in range(4)
    }
    for d in (1, 2, 3):
        back_y[d].start()
    last[0].start()
    for d in (1, 2, 3):
        back_y[4 - d].wait_recv()
        last[d].start()

    @pl.when(has_above)
    def _():
        lower.wait_recv()

        def add(step, carry):
            rows = pl.ds(pl.multiple_of(step * CHUNK, CHUNK), CHUNK)
            for c in range(2):
                for j in range(4):
                    new_object[c, rows, part(j)] += below_in[c, j, rows] * inverse[j, rows]
            return carry

        lax.fori_loop(0, SIDE // CHUNK, add, 0)

    @pl.when(has_left)
    def _():
        right_lower.wait_recv()
        right_upper.wait_recv()

        def add(step, carry):
            rows = pl.ds(pl.multiple_of(step * CHUNK, CHUNK), CHUNK)
            for c in range(2):
                for j in range(2):
                    new_object[c, rows, part(j)] += right_in[c, j, rows] * inverse[j, rows]
            return carry

        lax.fori_loop(0, 512 // CHUNK, add, 0)

    for d in range(4):
        last[d].wait_recv()
    for m in range(MODES):
        for c in range(2):
            for j in range(2):
                new_probe[m, c, :, part(j)] = turned[2 * m + c, pl.ds(j * SIDE, SIDE)]

    pl.when(has_below)(corner.wait_send)
    pl.when(has_below)(lower.wait_send)
    pl.when(has_right)(right_lower.wait_send)
    pl.when(has_right)(right_upper.wait_send)
    for copies in (halves, outward, crossing, along, back_x, back_y, last):
        for copy in copies.values():
            copy.wait_send()


def finish(grid, probe_sum, tile, inverse_light, probe):
    vmem, anywhere = [pl.BlockSpec(memory_space=space) for space in (pltpu.VMEM, pl.ANY)]
    f32 = functools.partial(pltpu.VMEM, dtype=jnp.float32)
    dma = pltpu.SemaphoreType.DMA
    return pl.pallas_call(
        finish_kernel,
        out_shape=(
            jax.ShapeDtypeStruct(tile.shape, jnp.float32),
            jax.ShapeDtypeStruct(probe.shape, jnp.float32),
        ),
        in_specs=[anywhere] * 4 + [vmem],
        out_specs=(vmem, vmem),
        scratch_shapes=[
            f32((2, 4, 512, HALF)),
            f32((5, 256, HALF)),
            f32((4, 512, HALF)),
            f32((2, 512, 512)),
            f32((2, 2, 256, HALF)),
            f32((2, 4, 256, HALF)),
            f32((2, 2, 512, HALF)),
            f32((2, 2, 256, HALF)),
            f32((5, 256, HALF)),
            f32((3, 5, 64, HALF)),
            f32((3, 5, 16, HALF)),
            f32((4, 5, 16, HALF)),
            f32((4, 512, HALF)),
            dma((5,)), dma((4,)), dma((4,)), dma((4,)), dma((4,)),
            *[dma((3,))] * 10,
            dma((4,)), dma((4,)),
        ],
        compiler_params=pltpu.CompilerParams(
            collective_id=0, has_side_effects=True, vmem_limit_bytes=VMEM_LIMIT
        ),
        name="finish",
    )(grid, probe_sum, tile, inverse_light, probe)


def shift_up(array, axis):
    count = lax.axis_size(axis)
    return lax.ppermute(array, axis, [(i, i - 1) for i in range(1, count)])


def shift_down(array, axis):
    count = lax.axis_size(axis)
    return lax.ppermute(array, axis, [(i, i + 1) for i in range(count - 1)])


def body(object_field, probe, amplitudes, positions, counts):
    tile_rows, tile_cols = object_field.shape[1:]
    right_upper = shift_up(object_field[:, :SIDE, :SIDE], "col")
    right_lower = shift_up(object_field[:, SIDE:, :SIDE], "col")
    lower_rim = shift_up(object_field[:, :SIDE, :], "row")
    corner_rim = shift_up(right_upper, "row")

    origin = jnp.stack([lax.axis_index("row") * tile_rows, lax.axis_index("col") * tile_cols])
    scans = jnp.concatenate([positions.reshape(-1), counts])
    scans = jnp.stack([scans, shift_down(scans, "col")])
    scans = jnp.concatenate([scans, shift_down(scans, "row")])
    corners = scans[:, :-1].reshape(4, -1, 2) - origin
    inverse_light, by_parity = prepare(corners, scans[:, -1], probe, amplitudes)

    span = jnp.stack([jnp.zeros((), jnp.int32), counts[0]])
    order = jnp.arange(positions.shape[0], dtype=jnp.int32)
    grid, probe_sum = patterns(
        span, order, corners[0], object_field, right_upper, right_lower, lower_rim, corner_rim, probe, by_parity
    )
    return finish(grid, probe_sum, object_field, inverse_light, probe)


def solution(mesh):
    in_specs = (
        P(None, "row", "col"),
        P(),
        P(("row", "col"), None, None),
        P(("row", "col"), None),
        P(("row", "col")),
    )
    out_specs = (P(None, "row", "col"), P())
    return jax.shard_map(body, mesh=mesh, in_specs=in_specs, out_specs=out_specs, check_vma=False)
```

```python
import functools

import jax
import jax.numpy as jnp
import ml_dtypes
import numpy as np
from jax import lax
from jax.experimental import pallas as pl
from jax.experimental.pallas import tpu as pltpu
from jax.sharding import PartitionSpec as P

SIDE = 256
HALF = 128
MODES = 2
CHUNK = 32
VMEM_LIMIT = 56 * 1024 * 1024


def dft_tables():
    point = np.arange(HALF)[:, None]
    tables = []
    for odd in (0, 1):
        angle = 2.0 * np.pi * ((point * (2 * np.arange(HALF)[None, :] + odd)) % SIDE) / SIDE
        cosine, sine = np.cos(angle) / 16.0, np.sin(angle) / 16.0
        table = np.block([[cosine, -sine], [sine, cosine]]).astype(np.float32)
        tables += [table, table.T]
    return np.stack(tables)


def split(value):
    high = value.astype(jnp.bfloat16)
    return high, (value - high.astype(jnp.float32)).astype(jnp.bfloat16)


def dot(left, right):
    return jnp.dot(left, right, preferred_element_type=jnp.float32)


def part(index):
    return pl.ds(index * HALF, HALF)


def pattern_kernel(
    positions, counts, tile, right_rim, lower_rim, probe_in, amplitude_in, tables_in, grid, probe_sum,
    extended, probe, amplitude, tables, right_table, left_table, sems,
    patch, rows_in, rows_out, columns_in, columns_out,
):
    copies = [(tile.at[c, :, part(j)], extended.at[c, j, pl.ds(0, 512)]) for c in range(2) for j in range(4)]
    copies.append((right_rim, extended.at[:, pl.ds(4, 2)]))
    copies.append((lower_rim, extended.at[:, pl.ds(0, 4), pl.ds(512, 256)]))
    copies += [(tables_in, tables), (probe_in, probe), (amplitude_in, amplitude)]
    copies = [pltpu.make_async_copy(a, b, sems.at[k]) for k, (a, b) in enumerate(copies)]
    for copy in copies[-3:] + copies[:-3]:
        copy.start()
    grid[...] = jnp.zeros_like(grid)
    probe_sum[...] = jnp.zeros_like(probe_sum)
    copies[-3].wait()
    for k in range(4):
        high, low = split(tables[k])
        for piece, value in enumerate((high, high, low)):
            right_table[k, pl.ds(piece * SIDE, SIDE)] = value
        for piece, value in enumerate((high, low, high)):
            left_table[k ^ 1, :, pl.ds(piece * SIDE, SIDE)] = value
    for copy in copies[:-3] + copies[-2:]:
        copy.wait()

    lane = lax.broadcasted_iota(jnp.int32, (CHUNK, HALF), 1)

    row_start, col_start = lax.axis_index("row") * 512, lax.axis_index("col") * 512

    def phases(slot, live, patch, rows_in, rows_out, columns_in, columns_out):
        top = positions[slot, 0] - row_start
        left = positions[slot, 1] - col_start
        first = left // HALF
        shift = lax.rem(left, HALF)
        back_shift = lax.rem(HALF - shift, HALF)

        def load(step, carry):
            r = pl.multiple_of(step * CHUNK, CHUNK)
            rows = pl.ds(r, CHUNK)
            pixels = []
            for c in range(2):
                tiles = [
                    pltpu.roll(extended[c, first + j, pl.ds(top + r, CHUNK), :], back_shift, 1) for j in range(3)
                ]
                pair = [jnp.where(lane < HALF - shift, tiles[j], tiles[j + 1]) for j in range(2)]
                for j in range(2):
                    patch[c, rows, part(j)] = pair[j]
                pixels.append(pair)
            for j in range(2):
                probe_sum[4, pl.ds(j * SIDE + r, CHUNK), :] += live * (pixels[0][j] * pixels[0][j] + pixels[1][j] * pixels[1][j])
            for m in range(MODES):
                real, imag = [], []
                for j in range(2):
                    probe_real, probe_imag = probe[m, 0, rows, part(j)], probe[m, 1, rows, part(j)]
                    real.append(probe_real * pixels[0][j] - probe_imag * pixels[1][j])
                    imag.append(probe_real * pixels[1][j] + probe_imag * pixels[0][j])
                at = pl.ds(pl.multiple_of(m * SIDE + r, CHUNK), CHUNK)
                for k, (first_half, second_half) in enumerate((real, imag)):
                    for odd, value in enumerate((first_half + second_half, first_half - second_half)):
                        high, low = split(value)
                        rows_in[odd, at, part(k)] = high
                        rows_in[odd, at, part(2 + k)] = low
            return carry

        lax.fori_loop(0, SIDE // CHUNK, load, 0, unroll=True)
        yield

        def along_rows(inverse):
            for odd in range(2):
                cut = rows_in[odd]
                cut = jnp.concatenate([cut, cut[:, :SIDE]], axis=1)
                rows_out[odd] = dot(cut, right_table[2 * odd + inverse])

        def along_columns(inverse):
            for odd in range(2):
                high, low = columns_in[odd, 0], columns_in[odd, 1]
                cut = jnp.concatenate([high, high, low], axis=0)
                columns_out[odd] = dot(left_table[2 * odd + inverse], cut)

        along_rows(0)
        yield

        def turn(step, carry):
            r = pl.multiple_of(step * CHUNK, CHUNK)
            for m in range(MODES):
                for odd in range(2):
                    for k in range(2):
                        upper = rows_out[odd, pl.ds(m * SIDE + r, CHUNK), part(k)]
                        lower = rows_out[odd, pl.ds(m * SIDE + HALF + r, CHUNK), part(k)]
                        for q, value in enumerate((upper + lower, upper - lower)):
                            high, low = split(value)
                            columns_in[q, 0, pl.ds(k * HALF + r, CHUNK), part(2 * m + odd)] = high
                            columns_in[q, 1, pl.ds(k * HALF + r, CHUNK), part(2 * m + odd)] = low
            return carry

        lax.fori_loop(0, HALF // CHUNK, turn, 0, unroll=True)
        yield
        along_columns(0)
        yield

        def scale(step, carry):
            r = pl.multiple_of(step * CHUNK, CHUNK)
            for q in range(2):
                for odd in range(2):
                    values = [
                        [columns_out[q, pl.ds(k * HALF + r, CHUNK), part(2 * m + odd)] for k in range(2)]
                        for m in range(MODES)
                    ]
                    intensity = sum(v * v for pair in values for v in pair)
                    measured = amplitude[slot, pl.ds(q * HALF + r, CHUNK), part(odd)]
                    factor = live * (measured * lax.rsqrt(jnp.maximum(intensity, 0.09)) - 1.0)
                    for m in range(MODES):
                        for k in range(2):
                            high, low = split(values[m][k] * factor)
                            columns_in[q, 0, pl.ds(k * HALF + r, CHUNK), part(2 * m + odd)] = high
                            columns_in[q, 1, pl.ds(k * HALF + r, CHUNK), part(2 * m + odd)] = low
            return carry

        lax.fori_loop(0, HALF // CHUNK, scale, 0, unroll=True)
        yield
        along_columns(1)
        yield

        def turn_back(step, carry):
            r = pl.multiple_of(step * CHUNK, CHUNK)
            for m in range(MODES):
                for odd in range(2):
                    for k in range(2):
                        even_sum = columns_out[0, pl.ds(k * HALF + r, CHUNK), part(2 * m + odd)]
                        odd_sum = columns_out[1, pl.ds(k * HALF + r, CHUNK), part(2 * m + odd)]
                        for q, value in enumerate((even_sum + odd_sum, even_sum - odd_sum)):
                            high, low = split(value)
                            at = pl.ds(m * SIDE + q * HALF + r, CHUNK)
                            rows_in[odd, at, part(k)] = high
                            rows_in[odd, at, part(2 + k)] = low
            return carry

        lax.fori_loop(0, HALF // CHUNK, turn_back, 0, unroll=True)
        yield
        along_rows(1)
        yield

        def gather(step, carry):
            r = pl.multiple_of(step * CHUNK, CHUNK)
            rows = pl.ds(r, CHUNK)
            real_grad, imag_grad = [0.0, 0.0], [0.0, 0.0]
            for m in range(MODES):
                at = pl.ds(pl.multiple_of(m * SIDE + r, CHUNK), CHUNK)
                even = [rows_out[0, at, part(k)] for k in range(2)]
                odd = [rows_out[1, at, part(k)] for k in range(2)]
                for j in range(2):
                    real, imag = [e + o if j == 0 else e - o for e, o in zip(even, odd)]
                    patch_real, patch_imag = patch[0, rows, part(j)], patch[1, rows, part(j)]
                    probe_sum[2 * m, pl.ds(j * SIDE + r, CHUNK), :] += patch_real * real + patch_imag * imag
                    probe_sum[2 * m + 1, pl.ds(j * SIDE + r, CHUNK), :] += patch_real * imag - patch_imag * real
                    probe_real, probe_imag = probe[m, 0, rows, part(j)], probe[m, 1, rows, part(j)]
                    real_grad[j] += probe_real * real + probe_imag * imag
                    imag_grad[j] += probe_real * imag - probe_imag * real
            for c, pair in enumerate((real_grad, imag_grad)):
                here, there = [pltpu.roll(value, shift, 1) for value in pair]
                tiles = (
                    jnp.where(lane >= shift, here, 0.0),
                    jnp.where(lane >= shift, there, here),
                    jnp.where(lane >= shift, 0.0, there),
                )
                for j in range(3):
                    grid[c, first + j, pl.ds(top + r, CHUNK), :] += tiles[j]
            return carry

        lax.fori_loop(0, SIDE // CHUNK, gather, 0, unroll=True)
        yield

    def visit(step, carry):
        pair = []
        for k in range(2):
            live = jnp.where(2 * step + k < counts[0], 1.0, 0.0)
            pair.append(phases(2 * step + k, live, *(buffer.at[k] for buffer in (patch, rows_in, rows_out, columns_in, columns_out))))
        next(pair[0])
        for _ in pair[0]:
            next(pair[1])
        for _ in pair[1]:
            pass
        return carry

    lax.fori_loop(0, (counts[0] + 1) // 2, visit, 0)


def patterns(positions, counts, tile, right_rim, lower_rim, probe, amplitude):
    tables = dft_tables()
    smem, vmem, anywhere = [pl.BlockSpec(memory_space=s) for s in (pltpu.SMEM, pltpu.VMEM, pl.ANY)]
    f32 = functools.partial(pltpu.VMEM, dtype=jnp.float32)
    bf16 = functools.partial(pltpu.VMEM, dtype=jnp.bfloat16)
    return pl.pallas_call(
        pattern_kernel,
        out_shape=(
            jax.ShapeDtypeStruct((2, 6, 768, HALF), jnp.float32),
            jax.ShapeDtypeStruct((5, 2 * SIDE, HALF), jnp.float32),
        ),
        in_specs=[smem] * 2 + [anywhere] * 6,
        out_specs=(vmem, vmem),
        scratch_shapes=[
            f32((2, 6, 768, HALF)),
            f32(probe.shape),
            f32(amplitude.shape),
            f32(tables.shape),
            bf16((4, 3 * SIDE, SIDE)),
            bf16((4, SIDE, 3 * SIDE)),
            pltpu.SemaphoreType.DMA((13,)),
            f32((2, 2, SIDE, SIDE)),
            bf16((2, 2, MODES * SIDE, 2 * SIDE)),
            f32((2, 2, MODES * SIDE, SIDE)),
            bf16((2, 2, 2, SIDE, MODES * SIDE)),
            f32((2, 2, SIDE, MODES * SIDE)),
        ],
        compiler_params=pltpu.CompilerParams(vmem_limit_bytes=VMEM_LIMIT),
        cost_estimate=pl.CostEstimate(flops=5_000_000_000, bytes_accessed=20_000_000, transcendentals=0),
        name="patterns",
    )(positions, counts, tile, right_rim, lower_rim, probe, amplitude, tables)


MESH_ID = pl.DeviceIdType.MESH


def remote(source, target, send, recv, device):
    return pltpu.make_async_remote_copy(
        src_ref=source, dst_ref=target, send_sem=send, recv_sem=recv, device_id=device, device_id_type=MESH_ID
    )


def rims_kernel(
    positions, counts, tile, probe, amplitude, right_rim, lower_rim, inverse_light, by_parity,
    parity, canvas, light, measured, reordered, columns, scan_in, scan, local_sems,
    upper_send, upper_recv, under_send, under_recv, lower_send, lower_recv, corner_send, corner_recv,
    scan_send, scan_recv,
):
    row, col = lax.axis_index("row"), lax.axis_index("col")
    has_above, has_below = row > 0, row < 7
    has_left, has_right = col > 0, col < 15
    above, below, left, right = (row - 1, col), (row + 1, col), (row, col - 1), (row, col + 1)
    partners = (
        (has_above, above), (has_below, below), (has_left, left), (has_right, right),
        (has_above & has_left, (row - 1, col - 1)), (has_below & has_right, (row + 1, col + 1)),
    )
    barrier = pltpu.get_barrier_semaphore()
    for there, device in partners:

        @pl.when(there)
        def _():
            pl.semaphore_signal(barrier, inc=1, device_id=device, device_id_type=MESH_ID)

    load = pltpu.make_async_copy(amplitude, measured, local_sems.at[1])
    load.start()
    slot_of = lax.broadcasted_iota(jnp.int32, (8, HALF), 0)
    field = lax.broadcasted_iota(jnp.int32, (8, HALF), 1)
    own_scan = jnp.where(slot_of < counts[0], 1, 0)
    for slot in range(8):
        for k in range(2):
            own_scan = jnp.where((slot_of == slot) & (field == k), positions[slot, k], own_scan)
    scan_in[0] = own_scan
    pl.semaphore_wait(barrier, sum(there.astype(jnp.int32) for there, _ in partners))

    pieces = [(c, j) for c in range(2) for j in range(2)]
    upper = [
        remote(
            tile.at[c, pl.ds(0, 256), part(j)], right_rim.at[c, j, pl.ds(0, 256)], upper_send.at[k], upper_recv.at[k], left
        )
        for k, (c, j) in enumerate(pieces)
    ]
    under = [
        remote(
            tile.at[c, pl.ds(256, 256), part(j)], right_rim.at[c, j, pl.ds(256, 256)],
            under_send.at[k], under_recv.at[k], left,
        )
        for k, (c, j) in enumerate(pieces)
    ]
    lower = [
        remote(
            tile.at[c, pl.ds(0, 256), part(j)], lower_rim.at[c, j],
            lower_send.at[4 * c + j], lower_recv.at[4 * c + j], above,
        )
        for c in range(2) for j in range(4)
    ]
    corner = remote(
        right_rim.at[:, :, pl.ds(0, 256)], right_rim.at[:, :, pl.ds(512, 256)],
        corner_send.at[0], corner_recv.at[0], above,
    )
    sources = (
        (has_right, right, has_left),
        (has_below, below, has_above),
        (has_below & has_right, (row + 1, col + 1), has_above & has_left),
    )
    passed = [
        remote(scan_in.at[0], scan_in.at[1 + k], scan_send.at[k], scan_recv.at[k], device)
        for k, (_, device, _) in enumerate(sources)
    ]

    @pl.when(has_left)
    def _():
        for copy in upper:
            copy.start()

    for copy, (there, _, arrives) in zip(passed, sources):
        pl.when(there)(copy.start)

    @pl.when(has_above)
    def _():
        for copy in lower:
            copy.start()

    @pl.when(has_left)
    def _():
        for copy in under:
            copy.start()

    line = lax.broadcasted_iota(jnp.int32, (3 * SIDE, SIDE), 0) % SIDE
    target = lax.broadcasted_iota(jnp.int32, (3 * SIDE, SIDE), 1)
    parity[...] = jnp.where(line == 2 * (target % HALF) + target // HALF, 1.0, 0.0).astype(jnp.bfloat16)
    load.wait()

    def reorder(slot, carry):
        for j in range(2):
            columns[j] = measured[slot, :, part(j)]
        for q in range(2):
            value = jnp.concatenate([columns[j, pl.ds(q, HALF, stride=2), :] for j in range(2)], axis=1)
            cut = []
            for _ in range(3):
                high = value.astype(jnp.bfloat16)
                cut.append(high)
                value = value - high.astype(jnp.float32)
            reordered[slot, part(q), :] = dot(jnp.concatenate(cut, axis=1), parity[...])
        return carry

    lax.fori_loop(0, 8, reorder, 0)
    stores = [pltpu.make_async_copy(reordered, by_parity, local_sems.at[1])]
    stores[0].start()

    canvas[...] = jnp.zeros_like(canvas)
    for j in range(2):
        canvas[4 + j, pl.ds(512, SIDE), :] = sum(probe[m, c, :, part(j)] * probe[m, c, :, part(j)] for m in range(MODES) for c in range(2))
    light[...] = jnp.zeros_like(light)
    for copy, (there, _, arrives), k in zip(passed, sources, range(1, 4)):
        pl.when(arrives)(copy.wait_recv)

        @pl.when(jnp.logical_not(arrives))
        def _():
            scan_in[k] = jnp.zeros_like(scan_in[k])

    to_scalars = pltpu.make_async_copy(scan_in, scan, local_sems.at[2])
    to_scalars.start()
    to_scalars.wait()
    lane = lax.broadcasted_iota(jnp.int32, (CHUNK, HALF), 1)

    def shine(source, height, width, slot, carry):
        top = scan[source, slot, 0] - row * 512
        start = 512 - (scan[source, slot, 1] - col * 512)
        live = scan[source, slot, 2] > 0
        top = jnp.where(live, 512 - top, 1024)
        start = jnp.where(live, start, 0)
        first = start // HALF
        shift = lax.rem(start, HALF)
        back_shift = lax.rem(HALF - shift, HALF)

        def rows_of(step, carry):
            r = pl.multiple_of(step * CHUNK, CHUNK)
            tiles = [pltpu.roll(canvas[first + j, pl.ds(top + r, CHUNK), :], back_shift, 1) for j in range(width + 1)]
            for j in range(width):
                light[j, pl.ds(r, CHUNK), :] += jnp.where(lane < HALF - shift, tiles[j], tiles[j + 1])
            return carry

        lax.fori_loop(0, height // CHUNK, rows_of, 0, unroll=4)
        return carry

    lax.fori_loop(0, 8, functools.partial(shine, 0, 512, 4), 0)

    @pl.when(has_right)
    def _():
        for copy in upper:
            copy.wait_recv()

    pl.when(has_right & has_above)(corner.start)

    lax.fori_loop(0, 8, functools.partial(shine, 1, 512, 2), 0)
    lax.fori_loop(0, 8, functools.partial(shine, 2, 256, 4), 0)
    lax.fori_loop(0, 8, functools.partial(shine, 3, 256, 2), 0)
    light[...] = 1.0 / (light[...] + 1.0)
    stores.append(pltpu.make_async_copy(light, inverse_light, local_sems.at[3]))
    stores[1].start()

    @pl.when(has_below)
    def _():
        for copy in lower:
            copy.wait_recv()

    @pl.when(has_right)
    def _():
        for copy in under:
            copy.wait_recv()

    pl.when(has_right & has_below)(corner.wait_recv)

    for store in stores:
        store.wait()
    for copy, (there, _, _) in zip(passed, sources):
        pl.when(there)(copy.wait_send)

    @pl.when(has_left)
    def _():
        for copy in upper + under:
            copy.wait_send()

    @pl.when(has_above)
    def _():
        for copy in lower:
            copy.wait_send()

    pl.when(has_right & has_above)(corner.wait_send)


def rims(positions, counts, tile, probe, amplitude):
    smem, vmem, anywhere = [pl.BlockSpec(memory_space=space) for space in (pltpu.SMEM, pltpu.VMEM, pl.ANY)]
    f32 = functools.partial(pltpu.VMEM, dtype=jnp.float32)
    dma = pltpu.SemaphoreType.DMA
    return pl.pallas_call(
        rims_kernel,
        out_shape=(
            jax.ShapeDtypeStruct((2, 2, 768, HALF), jnp.float32),
            jax.ShapeDtypeStruct((2, 4, 256, HALF), jnp.float32),
            jax.ShapeDtypeStruct((4, 512, HALF), jnp.float32),
            jax.ShapeDtypeStruct(amplitude.shape, jnp.float32),
        ),
        in_specs=[smem, smem, anywhere, vmem, anywhere],
        out_specs=(anywhere,) * 4,
        scratch_shapes=[
            pltpu.VMEM((3 * SIDE, SIDE), jnp.bfloat16),
            f32((13, 1536, HALF)),
            f32((4, 512, HALF)),
            f32(amplitude.shape),
            f32(amplitude.shape),
            f32((2, SIDE, HALF)),
            pltpu.VMEM((4, 8, HALF), jnp.int32),
            pltpu.SMEM((4, 8, HALF), jnp.int32),
            dma((4,)),
            dma((4,)), dma((4,)), dma((4,)), dma((4,)), dma((8,)), dma((8,)), dma((1,)), dma((1,)), dma((3,)), dma((3,)),
        ],
        compiler_params=pltpu.CompilerParams(
            collective_id=1, has_side_effects=True, vmem_limit_bytes=VMEM_LIMIT
        ),
        name="rims",
    )(positions, counts, tile, probe, amplitude)


def finish_kernel(
    grid, probe_sum, tile, inverse_light, probe, new_object, turned,
    own, own_half, inverse, old, corner_in, below_in, right_in, right_out, half_in, by_y, by_xz,
    local_sems, spill_send, spill_recv, half_send, half_recv, y_send, y_recv, xz_send, xz_recv,
    xz_back_send, xz_back_recv, y_back_send, y_back_recv, last_send, last_recv,
):
    row, col = lax.axis_index("row"), lax.axis_index("col")
    x, core = row // 2, lax.rem(row, 2)
    y, z = col // 4, lax.rem(col, 4)
    sibling = (row + 1 - 2 * core, col)
    y_peers = {d: (row, lax.rem(y + d, 4) * 4 + z) for d in (1, 2, 3)}
    xz_peers = {4 * dx + dz: (lax.rem(x + dx, 4) * 2 + core, y * 4 + lax.rem(z + dz, 4)) for dx in range(4) for dz in range(4)}
    del xz_peers[0]
    twin = x + 1 - 2 * lax.rem(x, 2)
    set_peers = {
        4 * flip + dz: ((twin if flip else x) * 2 + core, y * 4 + lax.rem(z + dz, 4)) for flip in range(2) for dz in range(4)
    }
    del set_peers[0]
    has_above, has_below = row > 0, row < 7
    has_left, has_right = col > 0, col < 15

    def signal(device):
        pl.semaphore_signal(barrier, inc=1, device_id=device, device_id_type=pl.DeviceIdType.MESH)

    half_at = core * 256
    loads = [
        pltpu.make_async_copy(probe_sum.at[:, pl.ds(pl.multiple_of(half_at, 256), 256)], own_half, local_sems.at[0]),
        pltpu.make_async_copy(grid.at[:, pl.ds(4, 2), pl.ds(0, 256)], right_out, local_sems.at[1]),
        pltpu.make_async_copy(grid.at[:, pl.ds(0, 4), pl.ds(0, 512)], own, local_sems.at[2]),
        pltpu.make_async_copy(inverse_light, inverse, local_sems.at[3]),
        pltpu.make_async_copy(tile, old, local_sems.at[4]),
    ]
    for load in loads:
        load.start()

    barrier = pltpu.get_barrier_semaphore()
    for device in [sibling, *y_peers.values(), *xz_peers.values()]:
        signal(device)
    steps = ((has_above, (row - 1, col)), (has_below, (row + 1, col)), (has_left, (row, col - 1)), (has_right, (row, col + 1)))
    for there, device in steps:
        pl.when(there)(functools.partial(signal, device))
    pl.semaphore_wait(barrier, 19 + sum(there.astype(jnp.int32) for there, _ in steps))

    below, right = (row + 1, col), (row, col + 1)
    corner = remote(
        grid.at[:, pl.ds(4, 2), pl.ds(512, 256)], corner_in, spill_send.at[0], spill_recv.at[0], below
    )
    right_lower = remote(
        grid.at[:, pl.ds(4, 2), pl.ds(256, 256)], right_in.at[:, :, pl.ds(256, 256)],
        spill_send.at[1], spill_recv.at[1], right,
    )
    lower = remote(grid.at[:, pl.ds(0, 4), pl.ds(512, 256)], below_in, spill_send.at[2], spill_recv.at[2], below)
    right_upper = remote(
        right_out, right_in.at[:, :, pl.ds(0, 256)], spill_send.at[3], spill_recv.at[3], right
    )

    def y_rows(d):
        return pl.ds(pl.multiple_of(lax.rem(y + d, 4) * 64, 64), 64)

    halves = {
        d: remote(
            probe_sum.at[:, pl.ds(pl.multiple_of((1 - core) * 256 + lax.rem(y + d, 4) * 64, 64), 64)],
            half_in.at[:, y_rows(d)], half_send.at[d], half_recv.at[d], sibling,
        )
        for d in range(4)
    }
    pl.when(has_below)(corner.start)
    for d in (2, 1, 3, 0):
        halves[d].start()
    pl.when(has_right)(right_lower.start)

    loads[0].wait()
    outward = {
        d: remote(own_half.at[:, y_rows(d)], by_y.at[3 - d], y_send.at[d - 1], y_recv.at[3 - d], y_peers[d])
        for d in (1, 2, 3)
    }
    for d in (2, 1, 3, 0):
        halves[d].wait_recv()
        own_half[:, y_rows(d)] = own_half[:, y_rows(d)] + half_in[:, y_rows(d)]
        if d:
            outward[d].start()

    loads[1].wait()

    @pl.when(has_above)
    def _():
        corner.wait_recv()
        right_out[...] = right_out[...] + corner_in[...]

    pl.when(has_right)(right_upper.start)
    pl.when(has_below)(lower.start)

    for d in (1, 2, 3):
        outward[d].wait_recv()
    mine = y_rows(0)
    own_half[:, mine] = own_half[:, mine] + (by_y[0] + by_y[1] + by_y[2])

    def eighth(index, base):
        return pl.ds(pl.multiple_of(base + index * 8, 8), 8)

    me, group = 4 * x + z, 4 * lax.rem(x, 2) + z
    crossing = {}
    for k, device in xz_peers.items():
        theirs = 4 * lax.rem(x + k // 4, 2) + lax.rem(z + k, 4)
        slot = 4 * ((4 - k // 4) % 4) + (4 - k % 4) % 4
        crossing[k] = remote(
            own_half.at[:, eighth(theirs, y * 64)], by_xz.at[me], xz_send.at[k], xz_recv.at[slot], device
        )
    for copy in crossing.values():
        copy.start()
    by_xz[me] = own_half[:, eighth(group, y * 64)]

    for load in loads[2:]:
        load.wait()

    def update(step, carry):
        rows = pl.ds(pl.multiple_of(step * CHUNK, CHUNK), CHUNK)
        for c in range(2):
            for j in range(4):
                new_object[c, rows, part(j)] = old[c, rows, part(j)] + own[c, j, rows] * inverse[j, rows]
        return carry

    lax.fori_loop(0, 512 // CHUNK, update, 0)

    for copy in crossing.values():
        copy.wait_recv()
    total = by_xz[0]
    for k in range(1, 16):
        total += by_xz[k]
    illumination = total[4] + 1.0
    pixels = eighth(group, y * 64)
    lanes = pl.ds(pl.multiple_of(core * HALF, HALF), HALF)
    home = eighth(group, half_at + y * 64)
    for m in range(MODES):
        for c in range(2):
            turned[2 * m + c, home] = probe[m, c, pixels, lanes] + total[2 * m + c] / illumination

    back_xz = {
        k: remote(
            turned.at[:, home], turned.at[:, home],
            xz_back_send.at[k], xz_back_recv.at[4 * (k // 4) + (4 - k % 4) % 4], device,
        )
        for k, device in set_peers.items()
    }
    for copy in back_xz.values():
        copy.start()
    for copy in back_xz.values():
        copy.wait_recv()

    def quarter(d):
        return pl.ds(pl.multiple_of(half_at + lax.rem(y + d, 4) * 64, 64), 64)

    back_y = {
        d: remote(
            turned.at[:, quarter(0)], turned.at[:, quarter(0)], y_back_send.at[d - 1], y_back_recv.at[3 - d], y_peers[d]
        )
        for d in (1, 2, 3)
    }
    last = {
        d: remote(turned.at[:, quarter(d)], turned.at[:, quarter(d)], last_send.at[d], last_recv.at[d], sibling)
        for d in range(4)
    }
    for d in (1, 2, 3):
        back_y[d].start()
    last[0].start()
    for d in (1, 2, 3):
        back_y[4 - d].wait_recv()
        last[d].start()

    @pl.when(has_above)
    def _():
        lower.wait_recv()

        def add(step, carry):
            rows = pl.ds(pl.multiple_of(step * CHUNK, CHUNK), CHUNK)
            for c in range(2):
                for j in range(4):
                    new_object[c, rows, part(j)] += below_in[c, j, rows] * inverse[j, rows]
            return carry

        lax.fori_loop(0, SIDE // CHUNK, add, 0)

    @pl.when(has_left)
    def _():
        right_lower.wait_recv()
        right_upper.wait_recv()

        def add(step, carry):
            rows = pl.ds(pl.multiple_of(step * CHUNK, CHUNK), CHUNK)
            for c in range(2):
                for j in range(2):
                    new_object[c, rows, part(j)] += right_in[c, j, rows] * inverse[j, rows]
            return carry

        lax.fori_loop(0, 512 // CHUNK, add, 0)

    for d in range(4):
        last[d].wait_recv()
    pl.when(has_below)(corner.wait_send)
    pl.when(has_below)(lower.wait_send)
    pl.when(has_right)(right_lower.wait_send)
    pl.when(has_right)(right_upper.wait_send)
    for copies in (halves, outward, crossing, back_xz, back_y, last):
        for copy in copies.values():
            copy.wait_send()


def finish(grid, probe_sum, tile, inverse_light, probe):
    vmem, anywhere = [pl.BlockSpec(memory_space=space) for space in (pltpu.VMEM, pl.ANY)]
    f32 = functools.partial(pltpu.VMEM, dtype=jnp.float32)
    dma = pltpu.SemaphoreType.DMA
    return pl.pallas_call(
        finish_kernel,
        out_shape=(
            jax.ShapeDtypeStruct(tile.shape, jnp.float32),
            jax.ShapeDtypeStruct((4, 2 * SIDE, HALF), jnp.float32),
        ),
        in_specs=[anywhere] * 4 + [vmem],
        out_specs=(vmem, vmem),
        scratch_shapes=[
            f32((2, 4, 512, HALF)),
            f32((5, 256, HALF)),
            f32((4, 512, HALF)),
            f32((2, 512, 512)),
            f32((2, 2, 256, HALF)),
            f32((2, 4, 256, HALF)),
            f32((2, 2, 512, HALF)),
            f32((2, 2, 256, HALF)),
            f32((5, 256, HALF)),
            f32((3, 5, 64, HALF)),
            f32((16, 5, 8, HALF)),
            dma((5,)), dma((4,)), dma((4,)), dma((4,)), dma((4,)),
            dma((3,)), dma((3,)), dma((16,)), dma((16,)), dma((8,)), dma((8,)), dma((3,)), dma((3,)), dma((4,)), dma((4,)),
        ],
        compiler_params=pltpu.CompilerParams(
            collective_id=0, has_side_effects=True, vmem_limit_bytes=VMEM_LIMIT
        ),
        name="finish",
    )(grid, probe_sum, tile, inverse_light, probe)


def publish_kernel(object_in, probe_in, new_object, new_probe):
    new_object[...] = object_in[...]
    for k in range(2 * MODES):
        for j in range(2):
            new_probe[k // 2, k % 2, :, part(j)] = probe_in[k, pl.ds(j * SIDE, SIDE)]


def publish(object_in, probe_in):
    vmem = pl.BlockSpec(memory_space=pltpu.VMEM)
    return pl.pallas_call(
        publish_kernel,
        out_shape=(
            jax.ShapeDtypeStruct(object_in.shape, jnp.float32),
            jax.ShapeDtypeStruct((MODES, 2, SIDE, SIDE), jnp.float32),
        ),
        in_specs=[vmem] * 2,
        out_specs=(vmem,) * 2,
        name="publish",
    )(object_in, probe_in)


def body(object_field, probe, amplitudes, positions, counts):
    right_rim, lower_rim, inverse_light, by_parity = rims(positions, counts, object_field, probe, amplitudes)
    grid, probe_sum = patterns(positions, counts, object_field, right_rim, lower_rim, probe, by_parity)
    return publish(*finish(grid, probe_sum, object_field, inverse_light, probe))


def solution(mesh):
    in_specs = (
        P(None, "row", "col"),
        P(),
        P(("row", "col"), None, None),
        P(("row", "col"), None),
        P(("row", "col")),
    )
    out_specs = (P(None, "row", "col"), P())
    return jax.shard_map(body, mesh=mesh, in_specs=in_specs, out_specs=out_specs, check_vma=False)
```

```python
import functools

import jax
import jax.numpy as jnp
import ml_dtypes
import numpy as np
from jax import lax
from jax.experimental import pallas as pl
from jax.experimental.pallas import tpu as pltpu
from jax.sharding import PartitionSpec as P

SIDE = 256
HALF = 128
MODES = 2
CHUNK = 32
VMEM_LIMIT = 56 * 1024 * 1024


def dft_tables():
    point = np.arange(HALF)[:, None]
    tables = []
    for odd in (0, 1):
        angle = 2.0 * np.pi * ((point * (2 * np.arange(HALF)[None, :] + odd)) % SIDE) / SIDE
        cosine, sine = np.cos(angle) / 16.0, np.sin(angle) / 16.0
        table = np.block([[cosine, -sine], [sine, cosine]]).astype(np.float32)
        tables += [table, table.T]
    return np.stack(tables)


def split(value):
    high = value.astype(jnp.bfloat16)
    return high, (value - high.astype(jnp.float32)).astype(jnp.bfloat16)


def dot(left, right):
    return jnp.dot(left, right, preferred_element_type=jnp.float32)


def part(index):
    return pl.ds(index * HALF, HALF)


def pattern_kernel(
    positions, counts, tile, right_rim, lower_rim, probe_in, amplitude_in, tables_in, grid, probe_sum,
    extended, probe, amplitude, tables, right_table, left_table, sems,
    patch, rows_in, rows_out, columns_in, columns_out,
):
    copies = [(tile.at[c, :, part(j)], extended.at[c, j, pl.ds(0, 512)]) for c in range(2) for j in range(4)]
    copies.append((right_rim, extended.at[:, pl.ds(4, 2)]))
    copies.append((lower_rim, extended.at[:, pl.ds(0, 4), pl.ds(512, 256)]))
    copies += [(tables_in, tables), (probe_in, probe), (amplitude_in, amplitude)]
    copies = [pltpu.make_async_copy(a, b, sems.at[k]) for k, (a, b) in enumerate(copies)]
    for copy in copies[-3:] + copies[:-3]:
        copy.start()
    grid[...] = jnp.zeros_like(grid)
    probe_sum[...] = jnp.zeros_like(probe_sum)
    copies[-3].wait()
    for k in range(4):
        high, low = split(tables[k])
        for piece, value in enumerate((high, high, low)):
            right_table[k, pl.ds(piece * SIDE, SIDE)] = value
        for piece, value in enumerate((high, low, high)):
            left_table[k ^ 1, :, pl.ds(piece * SIDE, SIDE)] = value
    for copy in copies[:-3] + copies[-2:]:
        copy.wait()

    lane = lax.broadcasted_iota(jnp.int32, (CHUNK, HALF), 1)

    row_start, col_start = lax.axis_index("row") * 512, lax.axis_index("col") * 512

    def phases(slot, live, patch, rows_in, rows_out, columns_in, columns_out):
        top = positions[0, slot] - row_start
        left = positions[1, slot] - col_start
        first = left // HALF
        shift = lax.rem(left, HALF)
        back_shift = lax.rem(HALF - shift, HALF)

        def load(step, carry):
            r = pl.multiple_of(step * CHUNK, CHUNK)
            rows = pl.ds(r, CHUNK)
            pixels = []
            for c in range(2):
                tiles = [
                    pltpu.roll(extended[c, first + j, pl.ds(top + r, CHUNK), :], back_shift, 1) for j in range(3)
                ]
                pair = [jnp.where(lane < HALF - shift, tiles[j], tiles[j + 1]) for j in range(2)]
                for j in range(2):
                    patch[c, rows, part(j)] = pair[j]
                pixels.append(pair)
            for j in range(2):
                probe_sum[4, pl.ds(j * SIDE + r, CHUNK), :] += live * (pixels[0][j] * pixels[0][j] + pixels[1][j] * pixels[1][j])
            for m in range(MODES):
                real, imag = [], []
                for j in range(2):
                    probe_real, probe_imag = probe[m, 0, rows, part(j)], probe[m, 1, rows, part(j)]
                    real.append(probe_real * pixels[0][j] - probe_imag * pixels[1][j])
                    imag.append(probe_real * pixels[1][j] + probe_imag * pixels[0][j])
                at = pl.ds(pl.multiple_of(m * SIDE + r, CHUNK), CHUNK)
                for k, (first_half, second_half) in enumerate((real, imag)):
                    for odd, value in enumerate((first_half + second_half, first_half - second_half)):
                        high, low = split(value)
                        rows_in[odd, at, part(k)] = high
                        rows_in[odd, at, part(2 + k)] = low
            return carry

        lax.fori_loop(0, SIDE // CHUNK, load, 0, unroll=True)
        yield

        def along_rows(inverse):
            for odd in range(2):
                cut = rows_in[odd]
                cut = jnp.concatenate([cut, cut[:, :SIDE]], axis=1)
                rows_out[odd] = dot(cut, right_table[2 * odd + inverse])

        def along_columns(inverse):
            for odd in range(2):
                high, low = columns_in[odd, 0], columns_in[odd, 1]
                cut = jnp.concatenate([high, high, low], axis=0)
                columns_out[odd] = dot(left_table[2 * odd + inverse], cut)

        along_rows(0)
        yield

        def turn(step, carry):
            r = pl.multiple_of(step * CHUNK, CHUNK)
            for m in range(MODES):
                for odd in range(2):
                    for k in range(2):
                        upper = rows_out[odd, pl.ds(m * SIDE + r, CHUNK), part(k)]
                        lower = rows_out[odd, pl.ds(m * SIDE + HALF + r, CHUNK), part(k)]
                        for q, value in enumerate((upper + lower, upper - lower)):
                            high, low = split(value)
                            columns_in[q, 0, pl.ds(k * HALF + r, CHUNK), part(2 * m + odd)] = high
                            columns_in[q, 1, pl.ds(k * HALF + r, CHUNK), part(2 * m + odd)] = low
            return carry

        lax.fori_loop(0, HALF // CHUNK, turn, 0, unroll=True)
        yield
        along_columns(0)
        yield

        def scale(step, carry):
            r = pl.multiple_of(step * CHUNK, CHUNK)
            for q in range(2):
                for odd in range(2):
                    values = [
                        [columns_out[q, pl.ds(k * HALF + r, CHUNK), part(2 * m + odd)] for k in range(2)]
                        for m in range(MODES)
                    ]
                    intensity = sum(v * v for pair in values for v in pair)
                    measured = amplitude[slot, pl.ds(q * HALF + r, CHUNK), part(odd)]
                    factor = live * (measured * lax.rsqrt(jnp.maximum(intensity, 0.09)) - 1.0)
                    for m in range(MODES):
                        for k in range(2):
                            high, low = split(values[m][k] * factor)
                            columns_in[q, 0, pl.ds(k * HALF + r, CHUNK), part(2 * m + odd)] = high
                            columns_in[q, 1, pl.ds(k * HALF + r, CHUNK), part(2 * m + odd)] = low
            return carry

        lax.fori_loop(0, HALF // CHUNK, scale, 0, unroll=True)
        yield
        along_columns(1)
        yield

        def turn_back(step, carry):
            r = pl.multiple_of(step * CHUNK, CHUNK)
            for m in range(MODES):
                for odd in range(2):
                    for k in range(2):
                        even_sum = columns_out[0, pl.ds(k * HALF + r, CHUNK), part(2 * m + odd)]
                        odd_sum = columns_out[1, pl.ds(k * HALF + r, CHUNK), part(2 * m + odd)]
                        for q, value in enumerate((even_sum + odd_sum, even_sum - odd_sum)):
                            high, low = split(value)
                            at = pl.ds(m * SIDE + q * HALF + r, CHUNK)
                            rows_in[odd, at, part(k)] = high
                            rows_in[odd, at, part(2 + k)] = low
            return carry

        lax.fori_loop(0, HALF // CHUNK, turn_back, 0, unroll=True)
        yield
        along_rows(1)
        yield

        def gather(step, carry):
            r = pl.multiple_of(step * CHUNK, CHUNK)
            rows = pl.ds(r, CHUNK)
            real_grad, imag_grad = [0.0, 0.0], [0.0, 0.0]
            for m in range(MODES):
                at = pl.ds(pl.multiple_of(m * SIDE + r, CHUNK), CHUNK)
                even = [rows_out[0, at, part(k)] for k in range(2)]
                odd = [rows_out[1, at, part(k)] for k in range(2)]
                for j in range(2):
                    real, imag = [e + o if j == 0 else e - o for e, o in zip(even, odd)]
                    patch_real, patch_imag = patch[0, rows, part(j)], patch[1, rows, part(j)]
                    probe_sum[2 * m, pl.ds(j * SIDE + r, CHUNK), :] += patch_real * real + patch_imag * imag
                    probe_sum[2 * m + 1, pl.ds(j * SIDE + r, CHUNK), :] += patch_real * imag - patch_imag * real
                    probe_real, probe_imag = probe[m, 0, rows, part(j)], probe[m, 1, rows, part(j)]
                    real_grad[j] += probe_real * real + probe_imag * imag
                    imag_grad[j] += probe_real * imag - probe_imag * real
            for c, pair in enumerate((real_grad, imag_grad)):
                here, there = [pltpu.roll(value, shift, 1) for value in pair]
                tiles = (
                    jnp.where(lane >= shift, here, 0.0),
                    jnp.where(lane >= shift, there, here),
                    jnp.where(lane >= shift, 0.0, there),
                )
                for j in range(3):
                    grid[c, first + j, pl.ds(top + r, CHUNK), :] += tiles[j]
            return carry

        lax.fori_loop(0, SIDE // CHUNK, gather, 0, unroll=True)
        yield

    def visit(step, carry):
        pair = []
        for k in range(2):
            live = jnp.where(2 * step + k < counts[0], 1.0, 0.0)
            pair.append(phases(2 * step + k, live, *(buffer.at[k] for buffer in (patch, rows_in, rows_out, columns_in, columns_out))))
        next(pair[0])
        for _ in pair[0]:
            next(pair[1])
        for _ in pair[1]:
            pass
        return carry

    lax.fori_loop(0, (counts[0] + 1) // 2, visit, 0)


def patterns(positions, counts, tile, right_rim, lower_rim, probe, amplitude):
    tables = dft_tables()
    smem, vmem, anywhere = [pl.BlockSpec(memory_space=s) for s in (pltpu.SMEM, pltpu.VMEM, pl.ANY)]
    f32 = functools.partial(pltpu.VMEM, dtype=jnp.float32)
    bf16 = functools.partial(pltpu.VMEM, dtype=jnp.bfloat16)
    return pl.pallas_call(
        pattern_kernel,
        out_shape=(
            jax.ShapeDtypeStruct((2, 6, 768, HALF), jnp.float32),
            jax.ShapeDtypeStruct((5, 2 * SIDE, HALF), jnp.float32),
        ),
        in_specs=[smem] * 2 + [anywhere] * 6,
        out_specs=(vmem, vmem),
        scratch_shapes=[
            f32((2, 6, 768, HALF)),
            f32(probe.shape),
            f32(amplitude.shape),
            f32(tables.shape),
            bf16((4, 3 * SIDE, SIDE)),
            bf16((4, SIDE, 3 * SIDE)),
            pltpu.SemaphoreType.DMA((13,)),
            f32((2, 2, SIDE, SIDE)),
            bf16((2, 2, MODES * SIDE, 2 * SIDE)),
            f32((2, 2, MODES * SIDE, SIDE)),
            bf16((2, 2, 2, SIDE, MODES * SIDE)),
            f32((2, 2, SIDE, MODES * SIDE)),
        ],
        compiler_params=pltpu.CompilerParams(vmem_limit_bytes=VMEM_LIMIT),
        cost_estimate=pl.CostEstimate(flops=5_000_000_000, bytes_accessed=20_000_000, transcendentals=0),
        name="patterns",
    )(positions, counts, tile, right_rim, lower_rim, probe, amplitude, tables)


MESH_ID = pl.DeviceIdType.MESH


def remote(source, target, send, recv, device):
    return pltpu.make_async_remote_copy(
        src_ref=source, dst_ref=target, send_sem=send, recv_sem=recv, device_id=device, device_id_type=MESH_ID
    )


def rims_kernel(
    positions, counts, tile, probe_in, amplitude, right_rim, lower_rim, inverse_light, by_parity,
    probe, parity, canvas, light, measured, reordered, columns, scan_in, scan, local_sems,
    upper_send, upper_recv, under_send, under_recv, lower_send, lower_recv, corner_send, corner_recv,
    scan_send, scan_recv,
):
    row, col = lax.axis_index("row"), lax.axis_index("col")
    has_above, has_below = row > 0, row < 7
    has_left, has_right = col > 0, col < 15
    above, below, left, right = (row - 1, col), (row + 1, col), (row, col - 1), (row, col + 1)
    partners = (
        (has_above, above), (has_below, below), (has_left, left), (has_right, right),
        (has_above & has_left, (row - 1, col - 1)), (has_below & has_right, (row + 1, col + 1)),
    )
    barrier = pltpu.get_barrier_semaphore()
    for there, device in partners:

        @pl.when(there)
        def _():
            pl.semaphore_signal(barrier, inc=1, device_id=device, device_id_type=MESH_ID)

    load = pltpu.make_async_copy(amplitude, measured, local_sems.at[1])
    load.start()
    probe_load = pltpu.make_async_copy(probe_in, probe, local_sems.at[0])
    probe_load.start()
    slot_of = lax.broadcasted_iota(jnp.int32, (8, HALF), 0)
    field = lax.broadcasted_iota(jnp.int32, (8, HALF), 1)
    own_scan = jnp.where(slot_of < counts[0], 1, 0)
    for slot in range(8):
        for k in range(2):
            own_scan = jnp.where((slot_of == slot) & (field == k), positions[k, slot], own_scan)
    scan_in[0] = own_scan
    pl.semaphore_wait(barrier, sum(there.astype(jnp.int32) for there, _ in partners))

    pieces = [(c, j) for c in range(2) for j in range(2)]
    upper = [
        remote(
            tile.at[c, pl.ds(0, 256), part(j)], right_rim.at[c, j, pl.ds(0, 256)], upper_send.at[k], upper_recv.at[k], left
        )
        for k, (c, j) in enumerate(pieces)
    ]
    under = [
        remote(
            tile.at[c, pl.ds(256, 256), part(j)], right_rim.at[c, j, pl.ds(256, 256)],
            under_send.at[k], under_recv.at[k], left,
        )
        for k, (c, j) in enumerate(pieces)
    ]
    lower = [
        remote(
            tile.at[c, pl.ds(0, 256), part(j)], lower_rim.at[c, j],
            lower_send.at[4 * c + j], lower_recv.at[4 * c + j], above,
        )
        for c in range(2) for j in range(4)
    ]
    corner = remote(
        right_rim.at[:, :, pl.ds(0, 256)], right_rim.at[:, :, pl.ds(512, 256)],
        corner_send.at[0], corner_recv.at[0], above,
    )
    sources = (
        (has_right, right, has_left),
        (has_below, below, has_above),
        (has_below & has_right, (row + 1, col + 1), has_above & has_left),
    )
    passed = [
        remote(scan_in.at[0], scan_in.at[1 + k], scan_send.at[k], scan_recv.at[k], device)
        for k, (_, device, _) in enumerate(sources)
    ]

    @pl.when(has_left)
    def _():
        for copy in upper:
            copy.start()

    for copy, (there, _, arrives) in zip(passed, sources):
        pl.when(there)(copy.start)

    @pl.when(has_above)
    def _():
        for copy in lower:
            copy.start()

    @pl.when(has_left)
    def _():
        for copy in under:
            copy.start()

    line = lax.broadcasted_iota(jnp.int32, (3 * SIDE, SIDE), 0) % SIDE
    target = lax.broadcasted_iota(jnp.int32, (3 * SIDE, SIDE), 1)
    parity[...] = jnp.where(line == 2 * (target % HALF) + target // HALF, 1.0, 0.0).astype(jnp.bfloat16)
    load.wait()

    def reorder(slot, carry):
        for j in range(2):
            columns[j] = measured[slot, :, part(j)]
        for q in range(2):
            value = jnp.concatenate([columns[j, pl.ds(q, HALF, stride=2), :] for j in range(2)], axis=1)
            cut = []
            for _ in range(3):
                high = value.astype(jnp.bfloat16)
                cut.append(high)
                value = value - high.astype(jnp.float32)
            reordered[slot, part(q), :] = dot(jnp.concatenate(cut, axis=1), parity[...])
        return carry

    lax.fori_loop(0, 8, reorder, 0)
    stores = [pltpu.make_async_copy(reordered, by_parity, local_sems.at[1])]
    stores[0].start()

    canvas[...] = jnp.zeros_like(canvas)
    probe_load.wait()
    for j in range(2):
        canvas[4 + j, pl.ds(512, SIDE), :] = sum(probe[m, c, :, part(j)] * probe[m, c, :, part(j)] for m in range(MODES) for c in range(2))
    light[...] = jnp.zeros_like(light)
    for copy, (there, _, arrives), k in zip(passed, sources, range(1, 4)):
        pl.when(arrives)(copy.wait_recv)

        @pl.when(jnp.logical_not(arrives))
        def _():
            scan_in[k] = jnp.zeros_like(scan_in[k])

    to_scalars = pltpu.make_async_copy(scan_in, scan, local_sems.at[2])
    to_scalars.start()
    to_scalars.wait()
    lane = lax.broadcasted_iota(jnp.int32, (CHUNK, HALF), 1)

    def shine(source, height, width, slot, carry):
        top = scan[source, slot, 0] - row * 512
        start = 512 - (scan[source, slot, 1] - col * 512)
        live = scan[source, slot, 2] > 0
        top = jnp.where(live, 512 - top, 1024)
        start = jnp.where(live, start, 0)
        first = start // HALF
        shift = lax.rem(start, HALF)
        back_shift = lax.rem(HALF - shift, HALF)

        def rows_of(step, carry):
            r = pl.multiple_of(step * CHUNK, CHUNK)
            tiles = [pltpu.roll(canvas[first + j, pl.ds(top + r, CHUNK), :], back_shift, 1) for j in range(width + 1)]
            for j in range(width):
                light[j, pl.ds(r, CHUNK), :] += jnp.where(lane < HALF - shift, tiles[j], tiles[j + 1])
            return carry

        lax.fori_loop(0, height // CHUNK, rows_of, 0, unroll=4)
        return carry

    lax.fori_loop(0, 8, functools.partial(shine, 0, 512, 4), 0)

    @pl.when(has_right)
    def _():
        for copy in upper:
            copy.wait_recv()

    pl.when(has_right & has_above)(corner.start)

    lax.fori_loop(0, 8, functools.partial(shine, 1, 512, 2), 0)
    lax.fori_loop(0, 8, functools.partial(shine, 2, 256, 4), 0)
    lax.fori_loop(0, 8, functools.partial(shine, 3, 256, 2), 0)
    light[...] = 1.0 / (light[...] + 1.0)
    stores.append(pltpu.make_async_copy(light, inverse_light, local_sems.at[3]))
    stores[1].start()

    @pl.when(has_below)
    def _():
        for copy in lower:
            copy.wait_recv()

    @pl.when(has_right)
    def _():
        for copy in under:
            copy.wait_recv()

    pl.when(has_right & has_below)(corner.wait_recv)

    for store in stores:
        store.wait()
    for copy, (there, _, _) in zip(passed, sources):
        pl.when(there)(copy.wait_send)

    @pl.when(has_left)
    def _():
        for copy in upper + under:
            copy.wait_send()

    @pl.when(has_above)
    def _():
        for copy in lower:
            copy.wait_send()

    pl.when(has_right & has_above)(corner.wait_send)


def rims(positions, counts, tile, probe, amplitude):
    smem, anywhere = [pl.BlockSpec(memory_space=space) for space in (pltpu.SMEM, pl.ANY)]
    f32 = functools.partial(pltpu.VMEM, dtype=jnp.float32)
    dma = pltpu.SemaphoreType.DMA
    return pl.pallas_call(
        rims_kernel,
        out_shape=(
            jax.ShapeDtypeStruct((2, 2, 768, HALF), jnp.float32),
            jax.ShapeDtypeStruct((2, 4, 256, HALF), jnp.float32),
            jax.ShapeDtypeStruct((4, 512, HALF), jnp.float32),
            jax.ShapeDtypeStruct(amplitude.shape, jnp.float32),
        ),
        in_specs=[smem, smem, anywhere, anywhere, anywhere],
        out_specs=(anywhere,) * 4,
        scratch_shapes=[
            f32(probe.shape),
            pltpu.VMEM((3 * SIDE, SIDE), jnp.bfloat16),
            f32((13, 1536, HALF)),
            f32((4, 512, HALF)),
            f32(amplitude.shape),
            f32(amplitude.shape),
            f32((2, SIDE, HALF)),
            pltpu.VMEM((4, 8, HALF), jnp.int32),
            pltpu.SMEM((4, 8, HALF), jnp.int32),
            dma((4,)),
            dma((4,)), dma((4,)), dma((4,)), dma((4,)), dma((8,)), dma((8,)), dma((1,)), dma((1,)), dma((3,)), dma((3,)),
        ],
        compiler_params=pltpu.CompilerParams(
            collective_id=1, has_side_effects=True, vmem_limit_bytes=VMEM_LIMIT
        ),
        name="rims",
    )(positions, counts, tile, probe, amplitude)


def finish_kernel(
    grid, probe_sum, tile, inverse_light, probe_in, new_object, turned,
    probe, own, own_half, inverse, old, corner_in, below_in, right_in, right_out, half_in, by_big, by_cross,
    local_sems, corner_send, corner_recv, right_send, right_recv, below_send, below_recv, half_send, half_recv, big_send, big_recv, cross_send, cross_recv,
    cross_back_send, cross_back_recv, big_back_send, big_back_recv, last_send, last_recv,
):
    row, col = lax.axis_index("row"), lax.axis_index("col")
    x, core = row // 2, lax.rem(row, 2)
    y, z = col // 4, lax.rem(col, 4)
    sibling = (row + 1 - 2 * core, col)
    big, other = x, y

    def at(b, o, c):
        return (b * 2 + core, o * 4 + c)

    big_peers = {d: at(lax.rem(big + d, 4), other, z) for d in (1, 2, 3)}
    cross_peers = {4 * d + dz: at(big, lax.rem(other + d, 4), lax.rem(z + dz, 4)) for d in range(4) for dz in range(4)}
    del cross_peers[0]
    twin = other + 1 - 2 * lax.rem(other, 2)
    set_peers = {4 * flip + dz: at(big, twin if flip else other, lax.rem(z + dz, 4)) for flip in range(2) for dz in range(4)}
    del set_peers[0]
    has_above, has_below = row > 0, row < 7
    has_left, has_right = col > 0, col < 15

    def signal(device):
        pl.semaphore_signal(barrier, inc=1, device_id=device, device_id_type=pl.DeviceIdType.MESH)

    half_at = core * 256
    loads = [
        pltpu.make_async_copy(probe_sum.at[:, pl.ds(pl.multiple_of(half_at, 256), 256)], own_half, local_sems.at[0]),
        pltpu.make_async_copy(grid.at[:, pl.ds(4, 2), pl.ds(0, 256)], right_out, local_sems.at[1]),
        pltpu.make_async_copy(grid.at[:, pl.ds(0, 4), pl.ds(0, 512)], own, local_sems.at[2]),
        pltpu.make_async_copy(inverse_light, inverse, local_sems.at[3]),
        pltpu.make_async_copy(tile, old, local_sems.at[4]),
        pltpu.make_async_copy(probe_in, probe, local_sems.at[5]),
    ]
    for load in loads:
        load.start()

    barrier = pltpu.get_barrier_semaphore()
    for device in [sibling, *big_peers.values(), *cross_peers.values()]:
        signal(device)
    steps = ((has_above, (row - 1, col)), (has_below, (row + 1, col)), (has_left, (row, col - 1)), (has_right, (row, col + 1)))
    for there, device in steps:
        pl.when(there)(functools.partial(signal, device))
    pl.semaphore_wait(barrier, 19 + sum(there.astype(jnp.int32) for there, _ in steps))

    below, right = (row + 1, col), (row, col + 1)
    corner = remote(
        grid.at[:, pl.ds(4, 2), pl.ds(512, 256)], corner_in, corner_send.at[0], corner_recv.at[0], below
    )
    to_right = []
    for k in range(4):
        rows = pl.ds(128 * k, 128)
        source = right_out.at[:, :, rows] if k < 2 else grid.at[:, pl.ds(4, 2), rows]
        to_right.append(remote(source, right_in.at[:, :, rows], right_send.at[k], right_recv.at[k], right))
    to_below = []
    for k in range(2):
        to_below.append(
            remote(
                grid.at[:, pl.ds(0, 4), pl.ds(512 + 128 * k, 128)], below_in.at[:, :, pl.ds(128 * k, 128)],
                below_send.at[k], below_recv.at[k], below,
            )
        )

    def big_rows(d):
        return pl.ds(pl.multiple_of(lax.rem(big + d, 4) * 64, 64), 64)

    halves = {
        d: remote(
            probe_sum.at[:, pl.ds(pl.multiple_of((1 - core) * 256 + lax.rem(big + d, 4) * 64, 64), 64)],
            half_in.at[:, big_rows(d)], half_send.at[d], half_recv.at[d], sibling,
        )
        for d in range(4)
    }
    pl.when(has_below)(corner.start)
    for d in (2, 1, 3, 0):
        halves[d].start()
    pl.when(has_right)(to_right[2].start)
    pl.when(has_right)(to_right[3].start)

    loads[0].wait()
    outward = {
        d: remote(own_half.at[:, big_rows(d)], by_big.at[3 - d], big_send.at[d - 1], big_recv.at[3 - d], big_peers[d])
        for d in (1, 2, 3)
    }
    for d in (2, 1, 3, 0):
        halves[d].wait_recv()
        own_half[:, big_rows(d)] = own_half[:, big_rows(d)] + half_in[:, big_rows(d)]
        if d:
            outward[d].start()
    pl.when(has_below)(to_below[0].start)
    pl.when(has_below)(to_below[1].start)

    loads[1].wait()

    @pl.when(has_above)
    def _():
        corner.wait_recv()
        right_out[...] = right_out[...] + corner_in[...]


    for d in (1, 2, 3):
        outward[d].wait_recv()
    mine = big_rows(0)
    own_half[:, mine] = own_half[:, mine] + (by_big[0] + by_big[1] + by_big[2])

    def eighth(index, base):
        return pl.ds(pl.multiple_of(base + index * 8, 8), 8)

    me, group = 4 * other + z, 4 * lax.rem(other, 2) + z
    crossing = {}
    for k, device in cross_peers.items():
        theirs = 4 * lax.rem(other + k // 4, 2) + lax.rem(z + k, 4)
        slot = 4 * ((4 - k // 4) % 4) + (4 - k % 4) % 4
        crossing[k] = remote(
            own_half.at[:, eighth(theirs, big * 64)], by_cross.at[me], cross_send.at[k], cross_recv.at[slot], device
        )
    for copy in crossing.values():
        copy.start()
    pl.when(has_right)(to_right[0].start)
    by_cross[me] = own_half[:, eighth(group, big * 64)]

    for load in loads[2:]:
        load.wait()

    def update(step, carry):
        rows = pl.ds(pl.multiple_of(step * CHUNK, CHUNK), CHUNK)
        for c in range(2):
            for j in range(4):
                new_object[c, rows, part(j)] = old[c, rows, part(j)] + own[c, j, rows] * inverse[j, rows]
        return carry

    lax.fori_loop(0, 512 // CHUNK, update, 0)

    for copy in crossing.values():
        copy.wait_recv()
    total = by_cross[0]
    for k in range(1, 16):
        total += by_cross[k]
    illumination = total[4] + 1.0
    pixels = eighth(group, big * 64)
    lanes = pl.ds(pl.multiple_of(core * HALF, HALF), HALF)
    home = eighth(group, half_at + big * 64)
    for m in range(MODES):
        for c in range(2):
            turned[2 * m + c, home] = probe[m, c, pixels, lanes] + total[2 * m + c] / illumination

    back_cross = {
        k: remote(
            turned.at[:, home], turned.at[:, home],
            cross_back_send.at[k], cross_back_recv.at[4 * (k // 4) + (4 - k % 4) % 4], device,
        )
        for k, device in set_peers.items()
    }
    for copy in back_cross.values():
        copy.start()
    pl.when(has_right)(to_right[1].start)
    for copy in back_cross.values():
        copy.wait_recv()

    def quarter(d):
        return pl.ds(pl.multiple_of(half_at + lax.rem(big + d, 4) * 64, 64), 64)

    back_big = {
        d: remote(
            turned.at[:, quarter(0)], turned.at[:, quarter(0)], big_back_send.at[d - 1], big_back_recv.at[3 - d], big_peers[d]
        )
        for d in (1, 2, 3)
    }
    last = {
        d: remote(turned.at[:, quarter(d)], turned.at[:, quarter(d)], last_send.at[d], last_recv.at[d], sibling)
        for d in range(4)
    }
    for d in (1, 2, 3):
        back_big[d].start()
    last[0].start()
    for d in (1, 2, 3):
        back_big[4 - d].wait_recv()
        last[d].start()

    @pl.when(has_above)
    def _():
        for copy in to_below:
            copy.wait_recv()

        def add(step, carry):
            rows = pl.ds(pl.multiple_of(step * CHUNK, CHUNK), CHUNK)
            for c in range(2):
                for j in range(4):
                    new_object[c, rows, part(j)] += below_in[c, j, rows] * inverse[j, rows]
            return carry

        lax.fori_loop(0, SIDE // CHUNK, add, 0)

    @pl.when(has_left)
    def _():
        for copy in to_right:
            copy.wait_recv()

        def add(step, carry):
            rows = pl.ds(pl.multiple_of(step * CHUNK, CHUNK), CHUNK)
            for c in range(2):
                for j in range(2):
                    new_object[c, rows, part(j)] += right_in[c, j, rows] * inverse[j, rows]
            return carry

        lax.fori_loop(0, 512 // CHUNK, add, 0)

    for d in range(4):
        last[d].wait_recv()
    pl.when(has_below)(corner.wait_send)
    for copy in to_below:
        pl.when(has_below)(copy.wait_send)
    for copy in to_right:
        pl.when(has_right)(copy.wait_send)
    for copies in (halves, outward, crossing, back_cross, back_big, last):
        for copy in copies.values():
            copy.wait_send()


def finish(grid, probe_sum, tile, inverse_light, probe):
    vmem, anywhere = [pl.BlockSpec(memory_space=space) for space in (pltpu.VMEM, pl.ANY)]
    f32 = functools.partial(pltpu.VMEM, dtype=jnp.float32)
    dma = pltpu.SemaphoreType.DMA
    return pl.pallas_call(
        finish_kernel,
        out_shape=(
            jax.ShapeDtypeStruct(tile.shape, jnp.float32),
            jax.ShapeDtypeStruct((4, 2 * SIDE, HALF), jnp.float32),
        ),
        in_specs=[anywhere] * 5,
        out_specs=(vmem, vmem),
        scratch_shapes=[
            f32(probe.shape),
            f32((2, 4, 512, HALF)),
            f32((5, 256, HALF)),
            f32((4, 512, HALF)),
            f32((2, 512, 512)),
            f32((2, 2, 256, HALF)),
            f32((2, 4, 256, HALF)),
            f32((2, 2, 512, HALF)),
            f32((2, 2, 256, HALF)),
            f32((5, 256, HALF)),
            f32((3, 5, 64, HALF)),
            f32((16, 5, 8, HALF)),
            dma((6,)), dma((1,)), dma((1,)), dma((4,)), dma((4,)), dma((2,)), dma((2,)), dma((4,)), dma((4,)),
            dma((3,)), dma((3,)), dma((16,)), dma((16,)), dma((8,)), dma((8,)), dma((3,)), dma((3,)), dma((4,)), dma((4,)),
        ],
        compiler_params=pltpu.CompilerParams(
            collective_id=0, has_side_effects=True, vmem_limit_bytes=VMEM_LIMIT
        ),
        name="finish",
    )(grid, probe_sum, tile, inverse_light, probe)


def publish_kernel(object_in, probe_in, new_object, new_probe):
    new_object[...] = object_in[...]
    for k in range(2 * MODES):
        for j in range(2):
            new_probe[k // 2, k % 2, :, part(j)] = probe_in[k, pl.ds(j * SIDE, SIDE)]


def publish(object_in, probe_in):
    vmem = pl.BlockSpec(memory_space=pltpu.VMEM)
    return pl.pallas_call(
        publish_kernel,
        out_shape=(
            jax.ShapeDtypeStruct(object_in.shape, jnp.float32),
            jax.ShapeDtypeStruct((MODES, 2, SIDE, SIDE), jnp.float32),
        ),
        in_specs=[vmem] * 2,
        out_specs=(vmem,) * 2,
        name="publish",
    )(object_in, probe_in)


def body(object_field, probe, amplitudes, positions, counts):
    positions = positions.T
    right_rim, lower_rim, inverse_light, by_parity = rims(positions, counts, object_field, probe, amplitudes)
    grid, probe_sum = patterns(positions, counts, object_field, right_rim, lower_rim, probe, by_parity)
    return publish(*finish(grid, probe_sum, object_field, inverse_light, probe))


def solution(mesh):
    in_specs = (
        P(None, "row", "col"),
        P(),
        P(("row", "col"), None, None),
        P(("row", "col"), None),
        P(("row", "col")),
    )
    out_specs = (P(None, "row", "col"), P())
    return jax.shard_map(body, mesh=mesh, in_specs=in_specs, out_specs=out_specs, check_vma=False)
```

```python
import functools

import jax
import jax.numpy as jnp
import ml_dtypes
import numpy as np
from jax import lax
from jax.experimental import pallas as pl
from jax.experimental.pallas import tpu as pltpu
from jax.sharding import PartitionSpec as P

SIDE = 256
HALF = 128
MODES = 2
CHUNK = 32
VMEM_LIMIT = 56 * 1024 * 1024


def dft_tables():
    point = np.arange(HALF)[:, None]
    tables = []
    for odd in (0, 1):
        angle = 2.0 * np.pi * ((point * (2 * np.arange(HALF)[None, :] + odd)) % SIDE) / SIDE
        cosine, sine = np.cos(angle) / 16.0, np.sin(angle) / 16.0
        table = np.block([[cosine, -sine], [sine, cosine]]).astype(np.float32)
        tables += [table, table.T]
    return np.stack(tables)


def split(value):
    high = value.astype(jnp.bfloat16)
    return high, (value - high.astype(jnp.float32)).astype(jnp.bfloat16)


def dot(left, right):
    return jnp.dot(left, right, preferred_element_type=jnp.float32)


def part(index):
    return pl.ds(index * HALF, HALF)


def pattern_kernel(
    positions, counts, tile, right_rim, lower_rim, probe_in, amplitude_in, tables_in, grid, probe_sum,
    extended, probe, amplitude, tables, right_table, left_table, sems,
    patch, rows_in, rows_out, columns_in, columns_out,
):
    copies = [(tile.at[c, :, part(j)], extended.at[c, j, pl.ds(0, 512)]) for c in range(2) for j in range(4)]
    copies.append((right_rim, extended.at[:, pl.ds(4, 2)]))
    copies.append((lower_rim, extended.at[:, pl.ds(0, 4), pl.ds(512, 256)]))
    copies += [(tables_in, tables), (probe_in, probe), (amplitude_in, amplitude)]
    copies = [pltpu.make_async_copy(a, b, sems.at[k]) for k, (a, b) in enumerate(copies)]
    for copy in copies[-3:] + copies[:-3]:
        copy.start()
    grid[...] = jnp.zeros_like(grid)
    probe_sum[...] = jnp.zeros_like(probe_sum)
    copies[-3].wait()
    for k in range(4):
        high, low = split(tables[k])
        for piece, value in enumerate((high, high, low)):
            right_table[k, pl.ds(piece * SIDE, SIDE)] = value
        for piece, value in enumerate((high, low, high)):
            left_table[k ^ 1, :, pl.ds(piece * SIDE, SIDE)] = value
    for copy in copies[:-3] + copies[-2:]:
        copy.wait()

    lane = lax.broadcasted_iota(jnp.int32, (CHUNK, HALF), 1)

    row_start, col_start = lax.axis_index("row") * 512, lax.axis_index("col") * 512

    def phases(slot, live, patch, rows_in, rows_out, columns_in, columns_out):
        top = positions[0, slot] - row_start
        left = positions[1, slot] - col_start
        first = left // HALF
        shift = lax.rem(left, HALF)
        back_shift = lax.rem(HALF - shift, HALF)

        def load(step, carry):
            r = pl.multiple_of(step * CHUNK, CHUNK)
            rows = pl.ds(r, CHUNK)
            pixels = []
            for c in range(2):
                tiles = [
                    pltpu.roll(extended[c, first + j, pl.ds(top + r, CHUNK), :], back_shift, 1) for j in range(3)
                ]
                pair = [jnp.where(lane < HALF - shift, tiles[j], tiles[j + 1]) for j in range(2)]
                for j in range(2):
                    patch[c, rows, part(j)] = pair[j]
                pixels.append(pair)
            for j in range(2):
                probe_sum[4, pl.ds(j * SIDE + r, CHUNK), :] += live * (pixels[0][j] * pixels[0][j] + pixels[1][j] * pixels[1][j])
            for m in range(MODES):
                real, imag = [], []
                for j in range(2):
                    probe_real, probe_imag = probe[m, 0, rows, part(j)], probe[m, 1, rows, part(j)]
                    real.append(probe_real * pixels[0][j] - probe_imag * pixels[1][j])
                    imag.append(probe_real * pixels[1][j] + probe_imag * pixels[0][j])
                at = pl.ds(pl.multiple_of(m * SIDE + r, CHUNK), CHUNK)
                for k, (first_half, second_half) in enumerate((real, imag)):
                    for odd, value in enumerate((first_half + second_half, first_half - second_half)):
                        high, low = split(value)
                        rows_in[odd, at, part(k)] = high
                        rows_in[odd, at, part(2 + k)] = low
            return carry

        lax.fori_loop(0, SIDE // CHUNK, load, 0, unroll=True)
        yield

        def along_rows(inverse):
            for odd in range(2):
                cut = rows_in[odd]
                cut = jnp.concatenate([cut, cut[:, :SIDE]], axis=1)
                rows_out[odd] = dot(cut, right_table[2 * odd + inverse])

        def along_columns(inverse):
            for odd in range(2):
                high, low = columns_in[odd, 0], columns_in[odd, 1]
                cut = jnp.concatenate([high, high, low], axis=0)
                columns_out[odd] = dot(left_table[2 * odd + inverse], cut)

        along_rows(0)
        yield

        def turn(step, carry):
            r = pl.multiple_of(step * CHUNK, CHUNK)
            for m in range(MODES):
                for odd in range(2):
                    for k in range(2):
                        upper = rows_out[odd, pl.ds(m * SIDE + r, CHUNK), part(k)]
                        lower = rows_out[odd, pl.ds(m * SIDE + HALF + r, CHUNK), part(k)]
                        for q, value in enumerate((upper + lower, upper - lower)):
                            high, low = split(value)
                            columns_in[q, 0, pl.ds(k * HALF + r, CHUNK), part(2 * m + odd)] = high
                            columns_in[q, 1, pl.ds(k * HALF + r, CHUNK), part(2 * m + odd)] = low
            return carry

        lax.fori_loop(0, HALF // CHUNK, turn, 0, unroll=True)
        yield
        along_columns(0)
        yield

        def scale(step, carry):
            r = pl.multiple_of(step * CHUNK, CHUNK)
            for q in range(2):
                for odd in range(2):
                    values = [
                        [columns_out[q, pl.ds(k * HALF + r, CHUNK), part(2 * m + odd)] for k in range(2)]
                        for m in range(MODES)
                    ]
                    intensity = sum(v * v for pair in values for v in pair)
                    measured = amplitude[slot, pl.ds(q * HALF + r, CHUNK), part(odd)]
                    factor = live * (measured * lax.rsqrt(jnp.maximum(intensity, 0.09)) - 1.0)
                    for m in range(MODES):
                        for k in range(2):
                            high, low = split(values[m][k] * factor)
                            columns_in[q, 0, pl.ds(k * HALF + r, CHUNK), part(2 * m + odd)] = high
                            columns_in[q, 1, pl.ds(k * HALF + r, CHUNK), part(2 * m + odd)] = low
            return carry

        lax.fori_loop(0, HALF // CHUNK, scale, 0, unroll=True)
        yield
        along_columns(1)
        yield

        def turn_back(step, carry):
            r = pl.multiple_of(step * CHUNK, CHUNK)
            for m in range(MODES):
                for odd in range(2):
                    for k in range(2):
                        even_sum = columns_out[0, pl.ds(k * HALF + r, CHUNK), part(2 * m + odd)]
                        odd_sum = columns_out[1, pl.ds(k * HALF + r, CHUNK), part(2 * m + odd)]
                        for q, value in enumerate((even_sum + odd_sum, even_sum - odd_sum)):
                            high, low = split(value)
                            at = pl.ds(m * SIDE + q * HALF + r, CHUNK)
                            rows_in[odd, at, part(k)] = high
                            rows_in[odd, at, part(2 + k)] = low
            return carry

        lax.fori_loop(0, HALF // CHUNK, turn_back, 0, unroll=True)
        yield
        along_rows(1)
        yield

        def gather(step, carry):
            r = pl.multiple_of(step * CHUNK, CHUNK)
            rows = pl.ds(r, CHUNK)
            real_grad, imag_grad = [0.0, 0.0], [0.0, 0.0]
            for m in range(MODES):
                at = pl.ds(pl.multiple_of(m * SIDE + r, CHUNK), CHUNK)
                even = [rows_out[0, at, part(k)] for k in range(2)]
                odd = [rows_out[1, at, part(k)] for k in range(2)]
                for j in range(2):
                    real, imag = [e + o if j == 0 else e - o for e, o in zip(even, odd)]
                    patch_real, patch_imag = patch[0, rows, part(j)], patch[1, rows, part(j)]
                    probe_sum[2 * m, pl.ds(j * SIDE + r, CHUNK), :] += patch_real * real + patch_imag * imag
                    probe_sum[2 * m + 1, pl.ds(j * SIDE + r, CHUNK), :] += patch_real * imag - patch_imag * real
                    probe_real, probe_imag = probe[m, 0, rows, part(j)], probe[m, 1, rows, part(j)]
                    real_grad[j] += probe_real * real + probe_imag * imag
                    imag_grad[j] += probe_real * imag - probe_imag * real
            for c, pair in enumerate((real_grad, imag_grad)):
                here, there = [pltpu.roll(value, shift, 1) for value in pair]
                tiles = (
                    jnp.where(lane >= shift, here, 0.0),
                    jnp.where(lane >= shift, there, here),
                    jnp.where(lane >= shift, 0.0, there),
                )
                for j in range(3):
                    grid[c, first + j, pl.ds(top + r, CHUNK), :] += tiles[j]
            return carry

        lax.fori_loop(0, SIDE // CHUNK, gather, 0, unroll=True)
        yield

    def visit(step, carry):
        pair = []
        for k in range(2):
            live = jnp.where(2 * step + k < counts[0], 1.0, 0.0)
            pair.append(phases(2 * step + k, live, *(buffer.at[k] for buffer in (patch, rows_in, rows_out, columns_in, columns_out))))
        next(pair[0])
        for _ in pair[0]:
            next(pair[1])
        for _ in pair[1]:
            pass
        return carry

    lax.fori_loop(0, (counts[0] + 1) // 2, visit, 0)


def patterns(positions, counts, tile, right_rim, lower_rim, probe, amplitude):
    tables = dft_tables()
    smem, vmem, anywhere = [pl.BlockSpec(memory_space=s) for s in (pltpu.SMEM, pltpu.VMEM, pl.ANY)]
    f32 = functools.partial(pltpu.VMEM, dtype=jnp.float32)
    bf16 = functools.partial(pltpu.VMEM, dtype=jnp.bfloat16)
    return pl.pallas_call(
        pattern_kernel,
        out_shape=(
            jax.ShapeDtypeStruct((2, 6, 768, HALF), jnp.float32),
            jax.ShapeDtypeStruct((5, 2 * SIDE, HALF), jnp.float32),
        ),
        in_specs=[smem] * 2 + [anywhere] * 6,
        out_specs=(vmem, vmem),
        scratch_shapes=[
            f32((2, 6, 768, HALF)),
            f32(probe.shape),
            f32(amplitude.shape),
            f32(tables.shape),
            bf16((4, 3 * SIDE, SIDE)),
            bf16((4, SIDE, 3 * SIDE)),
            pltpu.SemaphoreType.DMA((13,)),
            f32((2, 2, SIDE, SIDE)),
            bf16((2, 2, MODES * SIDE, 2 * SIDE)),
            f32((2, 2, MODES * SIDE, SIDE)),
            bf16((2, 2, 2, SIDE, MODES * SIDE)),
            f32((2, 2, SIDE, MODES * SIDE)),
        ],
        compiler_params=pltpu.CompilerParams(vmem_limit_bytes=VMEM_LIMIT),
        cost_estimate=pl.CostEstimate(flops=5_000_000_000, bytes_accessed=20_000_000, transcendentals=0),
        name="patterns",
    )(positions, counts, tile, right_rim, lower_rim, probe, amplitude, tables)


MESH_ID = pl.DeviceIdType.MESH


def remote(source, target, send, recv, device):
    return pltpu.make_async_remote_copy(
        src_ref=source, dst_ref=target, send_sem=send, recv_sem=recv, device_id=device, device_id_type=MESH_ID
    )


def rims_kernel(
    positions, counts, tile, probe_in, amplitude, right_rim, lower_rim, inverse_light, by_parity,
    probe, parity, canvas, light, measured, reordered, columns, scan_in, scan, local_sems,
    upper_send, upper_recv, under_send, under_recv, lower_send, lower_recv, corner_send, corner_recv,
    scan_send, scan_recv,
):
    row, col = lax.axis_index("row"), lax.axis_index("col")
    has_above, has_below = row > 0, row < 7
    has_left, has_right = col > 0, col < 15
    above, below, left, right = (row - 1, col), (row + 1, col), (row, col - 1), (row, col + 1)
    partners = (
        (has_above, above), (has_below, below), (has_left, left), (has_right, right),
        (has_above & has_left, (row - 1, col - 1)), (has_below & has_right, (row + 1, col + 1)),
    )
    barrier = pltpu.get_barrier_semaphore()
    for there, device in partners:

        @pl.when(there)
        def _():
            pl.semaphore_signal(barrier, inc=1, device_id=device, device_id_type=MESH_ID)

    load = pltpu.make_async_copy(amplitude, measured, local_sems.at[1])
    load.start()
    probe_load = pltpu.make_async_copy(probe_in, probe, local_sems.at[0])
    probe_load.start()
    slot_of = lax.broadcasted_iota(jnp.int32, (8, HALF), 0)
    field = lax.broadcasted_iota(jnp.int32, (8, HALF), 1)
    own_scan = jnp.where(slot_of < counts[0], 1, 0)
    for slot in range(8):
        for k in range(2):
            own_scan = jnp.where((slot_of == slot) & (field == k), positions[k, slot], own_scan)
    scan_in[0] = own_scan
    pl.semaphore_wait(barrier, sum(there.astype(jnp.int32) for there, _ in partners))

    pieces = [(c, j) for c in range(2) for j in range(2)]
    upper = [
        remote(
            tile.at[c, pl.ds(0, 256), part(j)], right_rim.at[c, j, pl.ds(0, 256)], upper_send.at[k], upper_recv.at[k], left
        )
        for k, (c, j) in enumerate(pieces)
    ]
    under = [
        remote(
            tile.at[c, pl.ds(256, 256), part(j)], right_rim.at[c, j, pl.ds(256, 256)],
            under_send.at[k], under_recv.at[k], left,
        )
        for k, (c, j) in enumerate(pieces)
    ]
    lower = [
        remote(
            tile.at[c, pl.ds(0, 256), part(j)], lower_rim.at[c, j],
            lower_send.at[4 * c + j], lower_recv.at[4 * c + j], above,
        )
        for c in range(2) for j in range(4)
    ]
    corner = remote(
        right_rim.at[:, :, pl.ds(0, 256)], right_rim.at[:, :, pl.ds(512, 256)],
        corner_send.at[0], corner_recv.at[0], above,
    )
    sources = (
        (has_right, right, has_left),
        (has_below, below, has_above),
        (has_below & has_right, (row + 1, col + 1), has_above & has_left),
    )
    passed = [
        remote(scan_in.at[0], scan_in.at[1 + k], scan_send.at[k], scan_recv.at[k], device)
        for k, (_, device, _) in enumerate(sources)
    ]

    @pl.when(has_left)
    def _():
        for copy in upper:
            copy.start()

    for copy, (there, _, arrives) in zip(passed, sources):
        pl.when(there)(copy.start)

    @pl.when(has_above)
    def _():
        for copy in lower:
            copy.start()

    @pl.when(has_left)
    def _():
        for copy in under:
            copy.start()

    line = lax.broadcasted_iota(jnp.int32, (3 * SIDE, SIDE), 0) % SIDE
    target = lax.broadcasted_iota(jnp.int32, (3 * SIDE, SIDE), 1)
    parity[...] = jnp.where(line == 2 * (target % HALF) + target // HALF, 1.0, 0.0).astype(jnp.bfloat16)
    load.wait()

    def reorder(slot, carry):
        for j in range(2):
            columns[j] = measured[slot, :, part(j)]
        for q in range(2):
            value = jnp.concatenate([columns[j, pl.ds(q, HALF, stride=2), :] for j in range(2)], axis=1)
            cut = []
            for _ in range(3):
                high = value.astype(jnp.bfloat16)
                cut.append(high)
                value = value - high.astype(jnp.float32)
            reordered[slot, part(q), :] = dot(jnp.concatenate(cut, axis=1), parity[...])
        return carry

    lax.fori_loop(0, 8, reorder, 0)
    stores = [pltpu.make_async_copy(reordered, by_parity, local_sems.at[1])]
    stores[0].start()

    canvas[...] = jnp.zeros_like(canvas)
    probe_load.wait()
    for j in range(2):
        canvas[4 + j, pl.ds(512, SIDE), :] = sum(probe[m, c, :, part(j)] * probe[m, c, :, part(j)] for m in range(MODES) for c in range(2))
    light[...] = jnp.zeros_like(light)
    for copy, (there, _, arrives), k in zip(passed, sources, range(1, 4)):
        pl.when(arrives)(copy.wait_recv)

        @pl.when(jnp.logical_not(arrives))
        def _():
            scan_in[k] = jnp.zeros_like(scan_in[k])

    to_scalars = pltpu.make_async_copy(scan_in, scan, local_sems.at[2])
    to_scalars.start()
    to_scalars.wait()
    lane = lax.broadcasted_iota(jnp.int32, (CHUNK, HALF), 1)

    def shine(source, height, width, slot, carry):
        top = scan[source, slot, 0] - row * 512
        start = 512 - (scan[source, slot, 1] - col * 512)
        live = scan[source, slot, 2] > 0
        top = jnp.where(live, 512 - top, 1024)
        start = jnp.where(live, start, 0)
        first = start // HALF
        shift = lax.rem(start, HALF)
        back_shift = lax.rem(HALF - shift, HALF)

        def rows_of(step, carry):
            r = pl.multiple_of(step * CHUNK, CHUNK)
            tiles = [pltpu.roll(canvas[first + j, pl.ds(top + r, CHUNK), :], back_shift, 1) for j in range(width + 1)]
            for j in range(width):
                light[j, pl.ds(r, CHUNK), :] += jnp.where(lane < HALF - shift, tiles[j], tiles[j + 1])
            return carry

        lax.fori_loop(0, height // CHUNK, rows_of, 0, unroll=4)
        return carry

    lax.fori_loop(0, 8, functools.partial(shine, 0, 512, 4), 0)

    @pl.when(has_right)
    def _():
        for copy in upper:
            copy.wait_recv()

    pl.when(has_right & has_above)(corner.start)

    lax.fori_loop(0, 8, functools.partial(shine, 1, 512, 2), 0)
    lax.fori_loop(0, 8, functools.partial(shine, 2, 256, 4), 0)
    lax.fori_loop(0, 8, functools.partial(shine, 3, 256, 2), 0)
    light[...] = 1.0 / (light[...] + 1.0)
    stores.append(pltpu.make_async_copy(light, inverse_light, local_sems.at[3]))
    stores[1].start()

    @pl.when(has_below)
    def _():
        for copy in lower:
            copy.wait_recv()

    @pl.when(has_right)
    def _():
        for copy in under:
            copy.wait_recv()

    pl.when(has_right & has_below)(corner.wait_recv)

    for store in stores:
        store.wait()
    for copy, (there, _, _) in zip(passed, sources):
        pl.when(there)(copy.wait_send)

    @pl.when(has_left)
    def _():
        for copy in upper + under:
            copy.wait_send()

    @pl.when(has_above)
    def _():
        for copy in lower:
            copy.wait_send()

    pl.when(has_right & has_above)(corner.wait_send)


def rims(positions, counts, tile, probe, amplitude):
    smem, anywhere = [pl.BlockSpec(memory_space=space) for space in (pltpu.SMEM, pl.ANY)]
    f32 = functools.partial(pltpu.VMEM, dtype=jnp.float32)
    dma = pltpu.SemaphoreType.DMA
    return pl.pallas_call(
        rims_kernel,
        out_shape=(
            jax.ShapeDtypeStruct((2, 2, 768, HALF), jnp.float32),
            jax.ShapeDtypeStruct((2, 4, 256, HALF), jnp.float32),
            jax.ShapeDtypeStruct((4, 512, HALF), jnp.float32),
            jax.ShapeDtypeStruct(amplitude.shape, jnp.float32),
        ),
        in_specs=[smem, smem, anywhere, anywhere, anywhere],
        out_specs=(anywhere,) * 4,
        scratch_shapes=[
            f32(probe.shape),
            pltpu.VMEM((3 * SIDE, SIDE), jnp.bfloat16),
            f32((13, 1536, HALF)),
            f32((4, 512, HALF)),
            f32(amplitude.shape),
            f32(amplitude.shape),
            f32((2, SIDE, HALF)),
            pltpu.VMEM((4, 8, HALF), jnp.int32),
            pltpu.SMEM((4, 8, HALF), jnp.int32),
            dma((4,)),
            dma((4,)), dma((4,)), dma((4,)), dma((4,)), dma((8,)), dma((8,)), dma((1,)), dma((1,)), dma((3,)), dma((3,)),
        ],
        compiler_params=pltpu.CompilerParams(
            collective_id=1, has_side_effects=True, vmem_limit_bytes=VMEM_LIMIT
        ),
        name="rims",
    )(positions, counts, tile, probe, amplitude)


def finish_kernel(
    grid, probe_sum, tile, inverse_light, probe_in, new_object, turned,
    probe, own, own_half, inverse, old, corner_in, below_in, right_in, right_out, half_in, by_big, by_cross,
    local_sems, corner_send, corner_recv, right_send, right_recv, below_send, below_recv, half_send, half_recv, big_send, big_recv, cross_send, cross_recv,
    cross_back_send, cross_back_recv, big_back_send, big_back_recv, last_send, last_recv,
):
    row, col = lax.axis_index("row"), lax.axis_index("col")
    x, core = row // 2, lax.rem(row, 2)
    y, z = col // 4, lax.rem(col, 4)
    sibling = (row + 1 - 2 * core, col)
    big, other = x, y

    def at(b, o, c):
        return (b * 2 + core, o * 4 + c)

    big_peers = {d: at(lax.rem(big + d, 4), other, z) for d in (1, 2, 3)}
    cross_peers = {4 * d + dz: at(big, lax.rem(other + d, 4), lax.rem(z + dz, 4)) for d in range(4) for dz in range(4)}
    del cross_peers[0]
    twin = other + 1 - 2 * lax.rem(other, 2)
    set_peers = {4 * flip + dz: at(big, twin if flip else other, lax.rem(z + dz, 4)) for flip in range(2) for dz in range(4)}
    del set_peers[0]
    has_above, has_below = row > 0, row < 7
    has_left, has_right = col > 0, col < 15

    def signal(device):
        pl.semaphore_signal(barrier, inc=1, device_id=device, device_id_type=pl.DeviceIdType.MESH)

    half_at = core * 256
    loads = [
        pltpu.make_async_copy(probe_sum.at[:, pl.ds(pl.multiple_of(half_at, 256), 256)], own_half, local_sems.at[0]),
        pltpu.make_async_copy(grid.at[:, pl.ds(4, 2), pl.ds(0, 256)], right_out, local_sems.at[1]),
        pltpu.make_async_copy(grid.at[:, pl.ds(0, 4), pl.ds(0, 512)], own, local_sems.at[2]),
        pltpu.make_async_copy(inverse_light, inverse, local_sems.at[3]),
        pltpu.make_async_copy(tile, old, local_sems.at[4]),
        pltpu.make_async_copy(probe_in, probe, local_sems.at[5]),
    ]
    for load in loads:
        load.start()

    barrier = pltpu.get_barrier_semaphore()
    for device in [sibling, *big_peers.values(), *cross_peers.values()]:
        signal(device)
    steps = ((has_above, (row - 1, col)), (has_below, (row + 1, col)), (has_left, (row, col - 1)), (has_right, (row, col + 1)))
    for there, device in steps:
        pl.when(there)(functools.partial(signal, device))
    pl.semaphore_wait(barrier, 19 + sum(there.astype(jnp.int32) for there, _ in steps))

    below, right = (row + 1, col), (row, col + 1)
    corner = remote(
        grid.at[:, pl.ds(4, 2), pl.ds(512, 256)], corner_in, corner_send.at[0], corner_recv.at[0], below
    )
    to_right = []
    for k in range(4):
        rows = pl.ds(128 * k, 128)
        source = right_out.at[:, :, rows] if k < 2 else grid.at[:, pl.ds(4, 2), rows]
        to_right.append(remote(source, right_in.at[:, :, rows], right_send.at[k], right_recv.at[k], right))
    to_below = []
    for k in range(2):
        to_below.append(
            remote(
                grid.at[:, pl.ds(0, 4), pl.ds(512 + 128 * k, 128)], below_in.at[:, :, pl.ds(128 * k, 128)],
                below_send.at[k], below_recv.at[k], below,
            )
        )

    def big_rows(d):
        return pl.ds(pl.multiple_of(lax.rem(big + d, 4) * 64, 64), 64)

    halves = {
        d: remote(
            probe_sum.at[:, pl.ds(pl.multiple_of((1 - core) * 256 + lax.rem(big + d, 4) * 64, 64), 64)],
            half_in.at[:, big_rows(d)], half_send.at[d], half_recv.at[d], sibling,
        )
        for d in range(4)
    }
    pl.when(has_below)(corner.start)
    for d in (2, 1, 3, 0):
        halves[d].start()
    pl.when(has_right)(to_right[2].start)
    pl.when(has_right)(to_right[3].start)

    loads[0].wait()
    outward = {
        d: remote(own_half.at[:, big_rows(d)], by_big.at[3 - d], big_send.at[d - 1], big_recv.at[3 - d], big_peers[d])
        for d in (1, 2, 3)
    }
    for d in (2, 1, 3, 0):
        halves[d].wait_recv()
        own_half[:, big_rows(d)] = own_half[:, big_rows(d)] + half_in[:, big_rows(d)]
        if d:
            outward[d].start()

    loads[1].wait()

    @pl.when(has_above)
    def _():
        corner.wait_recv()
        right_out[...] = right_out[...] + corner_in[...]


    for d in (1, 2, 3):
        outward[d].wait_recv()
    mine = big_rows(0)
    own_half[:, mine] = own_half[:, mine] + (by_big[0] + by_big[1] + by_big[2])

    def eighth(index, base):
        return pl.ds(pl.multiple_of(base + index * 8, 8), 8)

    me, group = 4 * other + z, 4 * lax.rem(other, 2) + z
    crossing = {}
    for k, device in cross_peers.items():
        theirs = 4 * lax.rem(other + k // 4, 2) + lax.rem(z + k, 4)
        slot = 4 * ((4 - k // 4) % 4) + (4 - k % 4) % 4
        crossing[k] = remote(
            own_half.at[:, eighth(theirs, big * 64)], by_cross.at[me], cross_send.at[k], cross_recv.at[slot], device
        )
    for copy in crossing.values():
        copy.start()
    pl.when(has_right)(to_right[0].start)
    pl.when(has_below)(to_below[0].start)
    pl.when(has_below)(to_below[1].start)
    by_cross[me] = own_half[:, eighth(group, big * 64)]

    for load in loads[2:]:
        load.wait()

    def update(step, carry):
        rows = pl.ds(pl.multiple_of(step * CHUNK, CHUNK), CHUNK)
        for c in range(2):
            for j in range(4):
                new_object[c, rows, part(j)] = old[c, rows, part(j)] + own[c, j, rows] * inverse[j, rows]
        return carry

    lax.fori_loop(0, 512 // CHUNK, update, 0)

    for copy in crossing.values():
        copy.wait_recv()
    total = by_cross[0]
    for k in range(1, 16):
        total += by_cross[k]
    illumination = total[4] + 1.0
    pixels = eighth(group, big * 64)
    lanes = pl.ds(pl.multiple_of(core * HALF, HALF), HALF)
    home = eighth(group, half_at + big * 64)
    for m in range(MODES):
        for c in range(2):
            turned[2 * m + c, home] = probe[m, c, pixels, lanes] + total[2 * m + c] / illumination

    back_cross = {
        k: remote(
            turned.at[:, home], turned.at[:, home],
            cross_back_send.at[k], cross_back_recv.at[4 * (k // 4) + (4 - k % 4) % 4], device,
        )
        for k, device in set_peers.items()
    }
    for copy in back_cross.values():
        copy.start()
    pl.when(has_right)(to_right[1].start)
    for copy in back_cross.values():
        copy.wait_recv()

    def quarter(d):
        return pl.ds(pl.multiple_of(half_at + lax.rem(big + d, 4) * 64, 64), 64)

    back_big = {
        d: remote(
            turned.at[:, quarter(0)], turned.at[:, quarter(0)], big_back_send.at[d - 1], big_back_recv.at[3 - d], big_peers[d]
        )
        for d in (1, 2, 3)
    }
    last = {
        d: remote(turned.at[:, quarter(d)], turned.at[:, quarter(d)], last_send.at[d], last_recv.at[d], sibling)
        for d in range(4)
    }
    for d in (1, 2, 3):
        back_big[d].start()
    last[0].start()
    for d in (1, 2, 3):
        back_big[4 - d].wait_recv()
        last[d].start()

    @pl.when(has_above)
    def _():
        for copy in to_below:
            copy.wait_recv()

        def add(step, carry):
            rows = pl.ds(pl.multiple_of(step * CHUNK, CHUNK), CHUNK)
            for c in range(2):
                for j in range(4):
                    new_object[c, rows, part(j)] += below_in[c, j, rows] * inverse[j, rows]
            return carry

        lax.fori_loop(0, SIDE // CHUNK, add, 0)

    @pl.when(has_left)
    def _():
        for copy in to_right:
            copy.wait_recv()

        def add(step, carry):
            rows = pl.ds(pl.multiple_of(step * CHUNK, CHUNK), CHUNK)
            for c in range(2):
                for j in range(2):
                    new_object[c, rows, part(j)] += right_in[c, j, rows] * inverse[j, rows]
            return carry

        lax.fori_loop(0, 512 // CHUNK, add, 0)

    for d in range(4):
        last[d].wait_recv()
    pl.when(has_below)(corner.wait_send)
    for copy in to_below:
        pl.when(has_below)(copy.wait_send)
    for copy in to_right:
        pl.when(has_right)(copy.wait_send)
    for copies in (halves, outward, crossing, back_cross, back_big, last):
        for copy in copies.values():
            copy.wait_send()


def finish(grid, probe_sum, tile, inverse_light, probe):
    vmem, anywhere = [pl.BlockSpec(memory_space=space) for space in (pltpu.VMEM, pl.ANY)]
    f32 = functools.partial(pltpu.VMEM, dtype=jnp.float32)
    dma = pltpu.SemaphoreType.DMA
    return pl.pallas_call(
        finish_kernel,
        out_shape=(
            jax.ShapeDtypeStruct(tile.shape, jnp.float32),
            jax.ShapeDtypeStruct((4, 2 * SIDE, HALF), jnp.float32),
        ),
        in_specs=[anywhere] * 5,
        out_specs=(vmem, vmem),
        scratch_shapes=[
            f32(probe.shape),
            f32((2, 4, 512, HALF)),
            f32((5, 256, HALF)),
            f32((4, 512, HALF)),
            f32((2, 512, 512)),
            f32((2, 2, 256, HALF)),
            f32((2, 4, 256, HALF)),
            f32((2, 2, 512, HALF)),
            f32((2, 2, 256, HALF)),
            f32((5, 256, HALF)),
            f32((3, 5, 64, HALF)),
            f32((16, 5, 8, HALF)),
            dma((6,)), dma((1,)), dma((1,)), dma((4,)), dma((4,)), dma((2,)), dma((2,)), dma((4,)), dma((4,)),
            dma((3,)), dma((3,)), dma((16,)), dma((16,)), dma((8,)), dma((8,)), dma((3,)), dma((3,)), dma((4,)), dma((4,)),
        ],
        compiler_params=pltpu.CompilerParams(
            collective_id=0, has_side_effects=True, vmem_limit_bytes=VMEM_LIMIT
        ),
        name="finish",
    )(grid, probe_sum, tile, inverse_light, probe)


def publish_kernel(object_in, probe_in, new_object, new_probe):
    new_object[...] = object_in[...]
    for k in range(2 * MODES):
        for j in range(2):
            new_probe[k // 2, k % 2, :, part(j)] = probe_in[k, pl.ds(j * SIDE, SIDE)]


def publish(object_in, probe_in):
    vmem = pl.BlockSpec(memory_space=pltpu.VMEM)
    return pl.pallas_call(
        publish_kernel,
        out_shape=(
            jax.ShapeDtypeStruct(object_in.shape, jnp.float32),
            jax.ShapeDtypeStruct((MODES, 2, SIDE, SIDE), jnp.float32),
        ),
        in_specs=[vmem] * 2,
        out_specs=(vmem,) * 2,
        name="publish",
    )(object_in, probe_in)


def body(object_field, probe, amplitudes, positions, counts):
    positions = positions.T
    right_rim, lower_rim, inverse_light, by_parity = rims(positions, counts, object_field, probe, amplitudes)
    grid, probe_sum = patterns(positions, counts, object_field, right_rim, lower_rim, probe, by_parity)
    return publish(*finish(grid, probe_sum, object_field, inverse_light, probe))


def solution(mesh):
    in_specs = (
        P(None, "row", "col"),
        P(),
        P(("row", "col"), None, None),
        P(("row", "col"), None),
        P(("row", "col")),
    )
    out_specs = (P(None, "row", "col"), P())
    return jax.shard_map(body, mesh=mesh, in_specs=in_specs, out_specs=out_specs, check_vma=False)
```
